512 devices in a mesh: slot: 64 (over y, z), tp: 8 (over x, core).
Axes of the slice: x: 4, y: 4, z: 16, core: 2. Of those that a mesh axis runs over, the one named last changes fastest.
Arguments:
- x_in: bfloat16 [49152, 8192], P('slot', 'tp'), may hold values from -6 to 6
- bc_in: bfloat16 [49152, 2048], P('slot', 'tp'), may hold values from -6 to 6
- z_gate: bfloat16 [49152, 8192], P('slot', 'tp'), may hold values from -60 to 60
- decay_rate: float32 [49152, 128], P('slot', 'tp'), may hold values from 0 to 2, as said below
- step_size: float32 [49152, 128], P('slot', 'tp'), may hold values from 0 to 1, as said below
- d_skip: float32 [128], P('tp'), may hold values from 0.5 to 1.5
- conv_x: float32 [4, 8192], P(None, 'tp'), may hold values from -3 to 3
- conv_bc: float32 [4, 2048], P(None, 'tp'), may hold values from -3 to 3
- norm_weight: float32 [8192], P('tp'), may hold values from 0.5 to 1.5
- lengths: int32 [4], replicated, may hold values from 1 to 24576, as said below
Outputs:
- gated_out: bfloat16 [49152, 8192], P('slot', 'tp')
The draws below stay inside these ranges and needn't reach their ends.
Inputs may be any that keep to these rules, and one draw needn't show every extreme that they name: prompt lengths in token order, laid end to end from token 0; the first prompt has 1536 to 12288 tokens and the second exactly 24576. `decay_rate`: positive. `step_size`: positive.
All inputs are finite; a program needn't handle non-finite values.
Results may differ from the reference program's by a relative error of at most 0.0055.
Values may be sent and summed in bfloat16 or wider, within the bound.
A program may use at most 128 MiB of HBM per device.

```python
import math
import jax
import jax.numpy as jnp
from jax import lax

SPACE_HEADS = 128
HEAD_DIM = 64
STATE = 128
GROUPS = 8
CONV = 4
SPAN = 768
TOK_DEV = 768
NDOC = 4
TOTAL_TOKENS = 49152


def head_base(key, share):
    random_keys = jax.random.split(key, 3)
    slow_heads = jax.random.uniform(random_keys[0], (SPACE_HEADS,)) < share
    slow_rate = jax.random.uniform(random_keys[1], (SPACE_HEADS,), minval=0.2, maxval=1.0) / TOTAL_TOKENS
    fast_rate = jnp.exp(jax.random.uniform(random_keys[2], (SPACE_HEADS,), minval=math.log(1.0 / 50.0), maxval=math.log(1.0 / 30.0)))
    return jnp.where(slow_heads, slow_rate, fast_rate)


def draw_decay_rate(key, part):
    baseline_rate = head_base(key, 0.5)
    rough_lo = 0.5
    rough_hi = 1.5
    key = jax.random.fold_in(key, 11)
    random_keys = jax.random.split(key, 4)
    jaggedness = jax.random.uniform(random_keys[0], (TOTAL_TOKENS, SPACE_HEADS), minval=rough_lo, maxval=rough_hi)
    shard_multiplier = jnp.exp(jax.random.uniform(random_keys[1], (TOTAL_TOKENS // TOK_DEV, SPACE_HEADS), minval=math.log(0.5), maxval=math.log(2.0)))
    shard_multiplier = jnp.repeat(shard_multiplier, TOK_DEV, axis=0)
    spike_position = jax.random.randint(random_keys[2], (3,), 0, TOTAL_TOKENS)
    spike_length = jax.random.uniform(random_keys[3], (3, SPACE_HEADS), minval=0.22, maxval=0.69)
    match_count = (jnp.arange(TOTAL_TOKENS, dtype=jnp.int32)[:, None] == spike_position[None, :]).astype(jnp.float32)
    spike_list = jnp.sum(match_count[:, :, None] * spike_length[None, :, :], axis=1)
    return baseline_rate[None, :] * shard_multiplier * jaggedness + spike_list


def draw_step_size(key, part):
    baseline_rate = head_base(key, 0.5)
    rough_lo = 0.5
    rough_hi = 1.5
    key = jax.random.fold_in(key, 12)
    jaggedness = jax.random.uniform(key, (TOTAL_TOKENS, SPACE_HEADS), minval=rough_lo, maxval=rough_hi)
    return jnp.sqrt(baseline_rate)[None, :] * jaggedness


def draw_z_gate(key, part):
    key = jax.random.fold_in(key, 13)
    random_keys = jax.random.split(key, 2)
    columns = SPACE_HEADS * HEAD_DIM
    column_scale = 0.5 * jnp.power(10.0, jnp.arange(columns, dtype=jnp.float32) / (columns - 1))
    row_scale = jnp.exp(jax.random.uniform(random_keys[1], (TOTAL_TOKENS, 1), minval=math.log(0.3), maxval=math.log(3.0)))
    values = jax.random.truncated_normal(random_keys[0], -4.0, 4.0, (TOTAL_TOKENS, columns))
    return (values * column_scale[None, :] * row_scale).astype(jnp.bfloat16)


def draw_lengths(key, part):
    key = jax.random.fold_in(key, 14)
    random_keys = jax.random.split(key, 2)
    first_len = jax.random.randint(random_keys[0], (1,), 2 * TOK_DEV, TOTAL_TOKENS // 4 + 1)
    longest = jnp.full((1,), TOTAL_TOKENS // 2, jnp.int32)
    remaining = TOTAL_TOKENS // 2 - first_len[0] - (NDOC - 2)
    cut_points = jnp.sort(jax.random.randint(random_keys[1], (NDOC - 3,), 0, remaining + 1))
    bounds = jnp.concatenate([jnp.zeros((1,), jnp.int32), cut_points.astype(jnp.int32), jnp.reshape(remaining, (1,)).astype(jnp.int32)])
    rest = bounds[1:] - bounds[:-1] + 1
    return jnp.concatenate([first_len.astype(jnp.int32), longest, rest.astype(jnp.int32)])


def block_levels(key, dims, shards, smallest, top_value):
    def one(position, parts):
        draws = jax.random.uniform(jax.random.fold_in(jax.random.fold_in(key, 6), position), (parts,), jnp.float32, smallest / len(shards), top_value / len(shards))
        return jnp.repeat(jnp.exp(draws), dims[position] // parts).reshape((-1,) + (1,) * (len(dims) - position - 1))

    loudness = one(*shards[0])
    for cut in shards[1:]:
        loudness = loudness * one(*cut)
    return loudness


def normal_values(rng, dims, width, most, cuts=(), held_as=jnp.bfloat16):
    loudness = block_levels(rng, dims, cuts, -0.22, 0.18) if cuts else 1.0
    array = jax.random.normal(rng, dims, jnp.float32) * width * loudness
    return jnp.minimum(jnp.maximum(array, -most), most).astype(held_as)


def setup_inputs(seed: int = 0) -> dict:
    splits = jax.random.split(jax.random.key(seed), 11)
    return {
        "x_in": normal_values(splits[0], (TOTAL_TOKENS, SPACE_HEADS * HEAD_DIM), 1.0, 6.0, ((0, 64), (1, 8))),
        "bc_in": normal_values(splits[1], (TOTAL_TOKENS, GROUPS * 2 * STATE), 1.0, 6.0, ((0, 64), (1, 8))),
        "z_gate": draw_z_gate(jax.random.fold_in(splits[10], 71), 0),
        "decay_rate": draw_decay_rate(jax.random.fold_in(splits[10], 71), 0),
        "step_size": draw_step_size(jax.random.fold_in(splits[10], 71), 0),
        "d_skip": jnp.clip(0.5 + 1.0 * jax.random.uniform(splits[5], (SPACE_HEADS,), jnp.float32) ** block_levels(splits[5], (SPACE_HEADS,), ((0, 8),), -0.2, 0.2), 0.5, 1.5),
        "conv_x": normal_values(splits[6], (CONV, SPACE_HEADS * HEAD_DIM), CONV ** -0.5, 3.0, ((1, 8),), jnp.float32),
        "conv_bc": normal_values(splits[7], (CONV, GROUPS * 2 * STATE), CONV ** -0.5, 3.0, ((1, 8),), jnp.float32),
        "norm_weight": jnp.clip(1.0 + 0.1 * jax.random.normal(splits[8], (SPACE_HEADS * HEAD_DIM,), jnp.float32), 0.5, 1.5),
        "lengths": draw_lengths(jax.random.fold_in(splits[10], 71), 0),
    }


EPSILON = 1e-05

def segment_of(positions, prompt_ends):
    return lax.optimization_barrier(jnp.sum((positions[:, None] >= prompt_ends[None, :]).astype(jnp.int32), axis=1, dtype=jnp.int32))

def conv_block(rim_rows, values_in, rim_seg, segment, weight):
    block_rows = values_in.shape[0]
    extended = jnp.concatenate([rim_rows, values_in], axis=0).astype(jnp.float32)
    ext_seg = jnp.concatenate([rim_seg, segment], axis=0)
    summed = weight[CONV - 1] * extended[CONV - 1:]
    for tap_index in range(CONV - 1):
        shifted = extended[tap_index:tap_index + block_rows]
        same_prompt = (ext_seg[tap_index:tap_index + block_rows] == segment)[:, None]
        summed = summed + weight[tap_index] * jnp.where(same_prompt, shifted, 0.0)
    return jax.nn.silu(summed).astype(jnp.bfloat16)

def span_terms(x_conv, bc_conv, rate_blk, step_blk, seg_blk, first_blk, d_skip):
    block_rows = x_conv.shape[0]
    head_count = rate_blk.shape[1]
    group_count = bc_conv.shape[1] // (2 * STATE)
    per_group = head_count // group_count
    head_vals = x_conv.reshape(block_rows, head_count, HEAD_DIM)
    paired = bc_conv.reshape(block_rows, group_count, 2, STATE)
    key_rows = paired[:, :, 0]
    queries = paired[:, :, 1]
    cum_rate = jnp.cumsum(rate_blk, axis=0)
    scores = jnp.einsum('tgn,sgn->gts', queries.astype(jnp.float32), key_rows.astype(jnp.float32))
    order_idx = jnp.arange(block_rows, dtype=jnp.int32)
    visible = (order_idx[:, None] >= order_idx[None, :]) & (seg_blk[:, None] == seg_blk[None, :])

    def pair_fn(pair_index):
        first_head = pair_index * 2
        group_index = first_head // per_group
        group_scores = lax.dynamic_index_in_dim(scores, group_index, 0, keepdims=False)
        cum_pair = lax.dynamic_slice_in_dim(cum_rate, first_head, 2, 1).T
        step_pair = lax.dynamic_slice_in_dim(step_blk, first_head, 2, 1).T
        differ = cum_pair[:, :, None] - cum_pair[:, None, :]
        decays = jnp.where(visible[None], jnp.exp(-jnp.where(visible[None], differ, 0.0)), 0.0)
        weights = (group_scores[None] * decays * step_pair[:, None, :]).astype(jnp.bfloat16)
        pair_vals = lax.dynamic_slice_in_dim(head_vals, first_head, 2, 1)
        return jnp.einsum('hts,shp->thp', weights.astype(jnp.float32), pair_vals.astype(jnp.float32))
    y_pairs = lax.map(pair_fn, jnp.arange(head_count // 2, dtype=jnp.int32))
    y_local = y_pairs.transpose(1, 0, 2, 3).reshape(block_rows, head_count, HEAD_DIM)
    y_local = y_local + d_skip[None, :, None] * head_vals.astype(jnp.float32)
    last_prompt = seg_blk[block_rows - 1]
    to_end = jnp.where((seg_blk == last_prompt)[:, None], jnp.exp(-(cum_rate[block_rows - 1][None, :] - cum_rate)), 0.0) * step_blk
    scaled = (to_end[:, :, None] * head_vals.astype(jnp.float32)).astype(jnp.bfloat16)
    state_local = jnp.einsum('sgrp,sgn->grpn', scaled.reshape(block_rows, group_count, per_group, HEAD_DIM).astype(jnp.float32), key_rows.astype(jnp.float32))
    state_local = state_local.reshape(head_count, HEAD_DIM, STATE)
    before_start = jnp.cumsum(first_blk.astype(jnp.int32), dtype=jnp.int32) == 0
    carry_in = jnp.where(before_start[:, None], jnp.exp(-cum_rate), 0.0)
    block_decay = jnp.where(jnp.any(first_blk), 0.0, jnp.exp(-cum_rate[block_rows - 1]))
    return (y_local, state_local, block_decay, carry_in, queries)

def add_carried(y_local, queries, carry_in, carried):
    block_rows, head_count = carry_in.shape
    group_count = queries.shape[1]
    carried_b = carried.astype(jnp.bfloat16).reshape(group_count, head_count // group_count, HEAD_DIM, STATE)
    carried_out = jnp.einsum('tgn,grpn->tgrp', queries.astype(jnp.float32), carried_b.astype(jnp.float32))
    return y_local + carry_in[:, :, None] * carried_out.reshape(block_rows, head_count, HEAD_DIM)

def gate_norm(y_full, z_blk, norm_weight):
    gated_rows = y_full.reshape(y_full.shape[0], -1) * jax.nn.silu(z_blk.astype(jnp.float32))
    mean_sq = lax.optimization_barrier(jnp.mean(gated_rows * gated_rows, axis=1, keepdims=True))
    return (gated_rows * lax.rsqrt(mean_sq + EPSILON) * norm_weight).astype(jnp.bfloat16)

def reference(x_in, bc_in, z_gate, decay_rate, step_size, d_skip, conv_x, conv_bc, norm_weight, lengths):
    positions = jnp.arange(TOTAL_TOKENS, dtype=jnp.int32)
    prompt_ends = jnp.cumsum(lengths, dtype=jnp.int32)
    prompt_starts = prompt_ends - lengths
    segment = segment_of(positions, prompt_ends)
    first_token = jnp.any(positions[:, None] == prompt_starts[None, :], axis=1)
    block_count = TOTAL_TOKENS // SPAN
    rim_width = CONV - 1

    def shape_blocks(values_in):
        return values_in.reshape((block_count, SPAN) + values_in.shape[1:])
    inputs = tuple((shape_blocks(item) for item in (x_in, bc_in, z_gate, decay_rate, step_size, segment, first_token)))
    start_carry = (jnp.zeros((SPACE_HEADS, HEAD_DIM, STATE), jnp.float32), jnp.zeros((rim_width, x_in.shape[1]), jnp.bfloat16), jnp.zeros((rim_width, bc_in.shape[1]), jnp.bfloat16), jnp.full((rim_width,), -1, jnp.int32))

    def advance(scan_carry, block_data):
        carried, rim_x, rim_bc, rim_seg = scan_carry
        x_blk, bc_blk, z_blk, rate_blk, step_blk, seg_blk, first_blk = block_data
        x_conv = conv_block(rim_x, x_blk, rim_seg, seg_blk, conv_x)
        bc_conv = conv_block(rim_bc, bc_blk, rim_seg, seg_blk, conv_bc)
        y_local, state_local, block_decay, carry_in, queries = span_terms(x_conv, bc_conv, rate_blk, step_blk, seg_blk, first_blk, d_skip)
        y_full = add_carried(y_local, queries, carry_in, carried)
        result = gate_norm(y_full, z_blk, norm_weight)
        new_state = block_decay[:, None, None] * carried + state_local
        next_carry = (new_state, x_blk[SPAN - rim_width:], bc_blk[SPAN - rim_width:], seg_blk[SPAN - rim_width:])
        return (next_carry, result)
    _, results = lax.scan(advance, start_carry, inputs)
    return results.reshape(TOTAL_TOKENS, SPACE_HEADS * HEAD_DIM)
```

```python
import functools

import jax
import jax.numpy as jnp
from jax import lax
from jax.experimental import pallas as pl
from jax.experimental.pallas import tpu as pltpu
from jax.sharding import PartitionSpec as P

MESH = pl.DeviceIdType.MESH
HEAD_DIM = 64
STATE = 128
SUB = 64
PARTS = 4
WIDE = 256
QUADS = 16
EPSILON = 1e-05
F32 = jnp.float32
BF16 = jnp.bfloat16


def silu(v):
    half = 0.5 * v
    return half * jnp.tanh(half) + half


def dot(a, b):
    return jnp.dot(a, b, preferred_element_type=F32)


def exact_dot(a, b, dims):
    return lax.dot_general(
        a, b, (dims, ((), ())), precision=lax.Precision.HIGHEST, preferred_element_type=F32
    )


def iota(shape, axis):
    return lax.broadcasted_iota(jnp.int32, shape, axis)


def two_terms(v):
    high = v.astype(BF16).astype(F32)
    return jnp.where(iota(v.shape, 1) < 16, high, v - high).astype(BF16)


def kernel(
    tp_size,
    len_ref,
    x_hbm,
    bc_ref,
    z_hbm,
    rate_ref,
    step_ref,
    skip_ref,
    conv_x_ref,
    conv_bc_ref,
    norm_ref,
    out_hbm,
    xs,
    zs,
    bcs,
    shift_ref,
    left_ref,
    right_ref,
    keys_ref,
    c_ref,
    xconv,
    cum_ref,
    mid_ref,
    end_ref,
    f_ref,
    e_ref,
    ef_ref,
    rows_ref,
    y_ref,
    g_ref,
    sq_ref,
    o_ref,
    decay_all,
    decay_rows,
    decay_wide,
    l_send,
    q_recv,
    t_send,
    o_recv,
    o_send,
    g_recv,
    p_send,
    c_recv,
    n_send,
    n_recv,
    n_rows,
    in_sem,
    out_sem,
    halo_send,
    halo_recv,
    d_send1,
    d_recv1,
    d_send2,
    d_recv2,
    s1,
    r1,
    s2,
    r2,
    s3,
    r3,
    s4,
    r4,
    ns,
    nr,
):
    tokens = x_hbm.shape[0]
    subs = tokens // SUB
    slots = 4 * QUADS
    slot = lax.axis_index("slot")
    tp = lax.axis_index("tp")
    quad = slot // 4
    member = slot % 4
    first_row = slot * tokens
    after, before = (slot + 1) % slots, (slot + slots - 1) % slots

    def quad_peer(i):
        return quad * 4 + (member + i) % 4

    def far_peer(i):
        return ((quad + i) % QUADS) * 4 + member

    def x_copy(p):
        return pltpu.make_async_copy(
            x_hbm.at[:, pl.ds(p * WIDE, WIDE)], xs.at[p, pl.ds(16, tokens)], in_sem.at[p]
        )

    def z_copy(p):
        return pltpu.make_async_copy(
            z_hbm.at[:, pl.ds(p * WIDE, WIDE)], zs.at[p], in_sem.at[PARTS + p]
        )

    barrier = pltpu.get_barrier_semaphore()

    def greet(peer):
        pl.semaphore_signal(barrier, inc=1, device_id={"slot": peer}, device_id_type=MESH)

    greet(after)
    greet(before)
    for i in range(1, 4):
        greet(quad_peer(i))
    lax.fori_loop(1, QUADS, lambda i, c: (greet(far_peer(i)), c)[1], 0)
    for i in range(1, tp_size):
        pl.semaphore_signal(
            barrier, inc=1, device_id={"tp": (tp + i) % tp_size}, device_id_type=MESH
        )
    for p in range(PARTS):
        x_copy(p).start()
    for p in range(PARTS):
        z_copy(p).start()

    ends = []
    total = 0
    for i in range(4):
        total = total + len_ref[i]
        ends.append(total)

    def start_of(pos, bounds):
        start = jnp.zeros_like(pos)
        for end in bounds:
            start = jnp.where(pos >= end, end, start)
        return start

    twice = (iota((16, 32), 0) == iota((16, 32), 1) % 16).astype(F32)
    zero_one = iota((128, 128), 0), iota((128, 128), 1)
    tri = ((zero_one[0] >= zero_one[1]) & (zero_one[0] // SUB == zero_one[1] // SUB)).astype(F32)
    width = min(128, tokens)
    for b in range(tokens // width):
        rate = rate_ref[b * width : (b + 1) * width, :]
        rate = jnp.concatenate([rate, rate], axis=1)
        cum_ref[b * width : (b + 1) * width, :] = exact_dot(
            tri[:width, :width], rate, ((1,), (0,))
        )
    mid_ref[...] = jnp.zeros_like(mid_ref)
    end_ref[...] = jnp.zeros_like(end_ref)
    offset = jnp.zeros((1, 32), F32)
    for c in range(subs):
        at = slice(c * SUB, (c + 1) * SUB)
        cum = cum_ref[at, :]
        mid = cum_ref[c * SUB + 31 : c * SUB + 32, :]
        end = cum_ref[c * SUB + 63 : c * SUB + 64, :]
        mid_ref[c : c + 1, :] = mid
        end_ref[c : c + 1, :] = end
        step = step_ref[at, :]
        step = jnp.concatenate([step, step], axis=1)
        f_ref[at, :] = two_terms(jnp.exp(cum - mid) * step)
        e_ref[at, :] = two_terms(jnp.exp(mid - cum))
        pos = first_row + c * SUB + iota((SUB, 32), 0)
        open_rows = start_of(pos, ends[:3]) < first_row
        ef_ref[at, :] = two_terms(jnp.where(open_rows, jnp.exp(-(offset + cum)), 0.0))
        offset = offset + end
    last_pos = first_row + tokens - 1 + jnp.zeros((1, 32), jnp.int32)
    whole = start_of(last_pos, ends[:3]) < first_row
    decay = jnp.where(whole, jnp.exp(-offset), 0.0)
    decay_all[slot] = jnp.zeros((1, 128), F32)
    decay_all[slot, :, 0:32] = jnp.where(iota((1, 32), 1) < 16, decay, 0.0)
    g1 = jnp.exp(-mid_ref[...])
    g2 = jnp.exp(mid_ref[...] - end_ref[...])
    sub_pos = first_row + iota((16, 32), 0) * SUB
    keep = start_of(sub_pos + (SUB - 1), ends) < sub_pos
    rows_ref[0:16, :] = two_terms(g1)
    rows_ref[16:32, :] = two_terms(g2)
    rows_ref[32:48, :] = two_terms(jnp.where(keep, g2, 0.0))
    skip = skip_ref[...]
    rows_ref[48:64, :] = two_terms(
        jnp.broadcast_to(jnp.concatenate([skip, skip], axis=1), (16, 32))
    )

    for c in range(subs):
        base = first_row + c * SUB
        t = iota((SUB, 80), 0)
        s = iota((SUB, 80), 1) - 16
        inside = (base + s) >= start_of(base + t, ends)
        for d in range(1, 4):
            shift_ref[c, (d - 1) * SUB : d * SUB, :] = ((s == t - d) & inside).astype(F32).astype(BF16)

    pl.semaphore_wait(barrier, 2 + 3 + (QUADS - 1) + (tp_size - 1))
    halos = []
    for p in range(PARTS):
        halos.append(
            pltpu.make_async_remote_copy(
                x_hbm.at[pl.ds(tokens - 16, 16), pl.ds(p * WIDE, WIDE)],
                xs.at[p, pl.ds(0, 16)],
                halo_send.at[p],
                halo_recv.at[p],
                device_id={"slot": after},
                device_id_type=MESH,
            )
        )
    halos.append(
        pltpu.make_async_remote_copy(
            bc_ref.at[pl.ds(tokens - 16, 16)],
            bcs.at[pl.ds(0, 16)],
            halo_send.at[PARTS],
            halo_recv.at[PARTS],
            device_id={"slot": after},
            device_id_type=MESH,
        )
    )
    halos[PARTS].start()
    for p in range(PARTS):
        halos[p].start()

    def near_decay(i):
        return pltpu.make_async_remote_copy(
            decay_all.at[slot],
            decay_all.at[slot],
            d_send1.at[i],
            d_recv1.at[i],
            device_id={"slot": quad_peer(i)},
            device_id_type=MESH,
        )

    def far_decay(i):
        return pltpu.make_async_remote_copy(
            decay_all.at[pl.ds(quad * 4, 4)],
            decay_all.at[pl.ds(quad * 4, 4)],
            d_send2.at[i],
            d_recv2.at[i],
            device_id={"slot": far_peer(i)},
            device_id_type=MESH,
        )

    for i in range(1, 4):
        near_decay(i).start()

    bcs[16:, :] = bc_ref[...]
    halos[PARTS].wait_recv()

    def conv(rows, shifts, taps):
        moved = dot(shifts, rows)
        summed = taps[3:4] * rows[16:].astype(F32)
        for d in range(1, 4):
            summed = summed + taps[3 - d : 4 - d] * moved[(d - 1) * SUB : d * SUB]
        return silu(summed).astype(BF16)

    for c in range(subs):
        base = first_row + c * SUB
        bc = conv(bcs[c * SUB : c * SUB + 80, :], shift_ref[c], conv_bc_ref[...])
        key, query = bc[:, :STATE], bc[:, STATE:]
        c_ref[c * SUB : (c + 1) * SUB, :] = query
        scores = lax.dot_general(query, key, (((1,), (1,)), ((), ())), preferred_element_type=F32)
        t = iota((SUB, SUB), 0)
        s = iota((SUB, SUB), 1)
        seen = (t >= s) & ((base + s) >= start_of(base + t, ends))
        left_ref[c, :, STATE:] = jnp.where(seen, scores, 0.0).astype(BF16)
        row = base + iota((SUB, STATE), 0)
        from_before = start_of(row, ends) < base
        left_ref[c, :, :STATE] = jnp.where(from_before, query.astype(F32), 0.0).astype(BF16)
        last = start_of(jnp.zeros((SUB, STATE), jnp.int32) + (base + SUB - 1), ends)
        keys = jnp.where(row >= last, key.astype(F32), 0.0)
        keys_ref[c] = keys.T.astype(BF16)

    for i in range(1, 4):
        near_decay(i).wait_recv()
    lax.fori_loop(1, QUADS, lambda i, c: (far_decay(i).start(), c)[1], 0)

    def widen_matrix(p, rows):
        r = iota((rows, WIDE), 0) % 16
        return (r == 4 * p + iota((rows, WIDE), 1) // HEAD_DIM).astype(F32).astype(BF16)

    def states(p):
        x_copy(p).wait()
        pltpu.make_async_remote_copy(
            x_hbm.at[pl.ds(tokens - 16, 16), pl.ds(0, WIDE)],
            xs.at[p, pl.ds(0, 16)],
            halo_send.at[p],
            halo_recv.at[p],
            device_id={"slot": after},
            device_id_type=MESH,
        ).wait_recv()
        taps = conv_x_ref[p]
        matrix = widen_matrix(p, 32)
        rows = dot(rows_ref[...], matrix)
        state = jnp.zeros((STATE, WIDE), F32)
        for c in range(subs):
            at = slice(c * SUB, (c + 1) * SUB)
            values = conv(xs[p, c * SUB : c * SUB + 80, :], shift_ref[c], taps)
            xconv[p, at, :] = values
            scaled = (values.astype(F32) * dot(f_ref[at, :], matrix)).astype(BF16)
            right_ref[p, c, STATE:, :] = scaled
            add = dot(keys_ref[c], scaled)
            if c == 0:
                right_ref[p, c, :STATE, :] = jnp.zeros((STATE, WIDE), BF16)
                state = rows[16 + c : 17 + c] * add
            else:
                faded = rows[c : c + 1] * state
                right_ref[p, c, :STATE, :] = faded.astype(BF16)
                state = rows[32 + c : 33 + c] * faded + rows[16 + c : 17 + c] * add
        l_send[p] = state.astype(BF16).reshape(4, 32, WIDE)

    def to_quad(p, i):
        return pltpu.make_async_remote_copy(
            l_send.at[p, (member + i) % 4],
            q_recv.at[p, member],
            s1.at[p, i],
            r1.at[p, i],
            device_id={"slot": quad_peer(i)},
            device_id_type=MESH,
        )

    def owner_of(p, tile):
        return 4 * tile + (p + 4 - tile) % 4

    def to_owner(p, tile):
        return pltpu.make_async_remote_copy(
            t_send.at[p, tile],
            o_recv.at[quad],
            s2.at[p, tile],
            r2.at[quad],
            device_id={"slot": owner_of(p, tile) * 4 + member},
            device_id_type=MESH,
        )

    my_part = (quad // 4 + quad % 4) % 4
    my_tile = quad // 4

    def from_owner(i):
        return pltpu.make_async_remote_copy(
            o_send.at[(quad + i) % QUADS],
            g_recv.at[my_part, my_tile],
            s3.at[i],
            r3.at[my_part, my_tile],
            device_id={"slot": far_peer(i)},
            device_id_type=MESH,
        )

    def to_member(p, i):
        return pltpu.make_async_remote_copy(
            p_send.at[p, (member + i) % 4],
            c_recv.at[p, member],
            s4.at[p, i],
            r4.at[p, i],
            device_id={"slot": quad_peer(i)},
            device_id_type=MESH,
        )

    def decay_of(p, i):
        row = pl.ds(quad * 4 + i, 1)
        return jnp.concatenate([decay_wide[2 * p, row, :], decay_wide[2 * p + 1, row, :]], axis=1)

    def quad_totals(p):
        for i in range(1, 4):
            to_quad(p, i).wait_recv()
        run = q_recv[p, 0].astype(F32)
        for i in range(1, 4):
            run = decay_of(p, i) * run + q_recv[p, i].astype(F32)
        run = run.astype(BF16)
        for tile in range(4):
            r, l = tile // 2, tile % 2
            t_send[p, tile] = run[16 * r : 16 * r + 16, 128 * l : 128 * l + 128]
        for tile in range(4):
            mine = owner_of(p, tile) == quad

            @pl.when(mine)
            def _():
                o_recv[quad] = t_send[p, tile]

            @pl.when(jnp.logical_not(mine))
            def _():
                to_owner(p, tile).start()

    def own():
        def wait_one(i, c):
            source = (quad + i) % QUADS
            pltpu.make_async_remote_copy(
                t_send.at[0, 0],
                o_recv.at[source],
                s2.at[0, 0],
                r2.at[source],
                device_id={"slot": far_peer(i)},
                device_id_type=MESH,
            ).wait_recv()
            return c

        lax.fori_loop(1, QUADS, wait_one, 0)
        tile = 2 * my_part + my_tile % 2
        run = jnp.zeros((16, 128), F32)
        for q in range(QUADS):
            o_send[q] = run.astype(BF16)
            fade = decay_wide[tile, 4 * q : 4 * q + 1, :]
            for i in range(1, 4):
                fade = fade * decay_wide[tile, 4 * q + i : 4 * q + i + 1, :]
            run = fade * run + o_recv[q].astype(F32)
        g_recv[my_part, my_tile] = o_send[quad]
        lax.fori_loop(1, QUADS, lambda i, c: (from_owner(i).start(), c)[1], 0)

    def members(p):
        for tile in range(4):

            @pl.when(owner_of(p, tile) != quad)
            def _():
                pltpu.make_async_remote_copy(
                    o_send.at[0],
                    g_recv.at[p, tile],
                    s3.at[0],
                    r3.at[p, tile],
                    device_id={"slot": after},
                    device_id_type=MESH,
                ).wait_recv()

        tiles = [g_recv[p, tile].astype(F32) for tile in range(4)]
        run = jnp.concatenate(
            [
                jnp.concatenate([tiles[0], tiles[1]], axis=1),
                jnp.concatenate([tiles[2], tiles[3]], axis=1),
            ],
            axis=0,
        )
        for i in range(4):
            p_send[p, i] = run.astype(BF16)
            if i < 3:
                run = decay_of(p, i) * run + q_recv[p, i].astype(F32)
        c_recv[p, member] = p_send[p, member]
        for i in range(1, 4):
            to_member(p, i).start()

    def local(p):
        z_copy(p).wait()
        matrix = widen_matrix(p, 32)
        skip_row = dot(rows_ref[48:64, :], matrix)[0:1]
        for c in range(subs):
            at = slice(c * SUB, (c + 1) * SUB)
            y = dot(left_ref[c], right_ref[p, c]) * dot(e_ref[at, :], matrix)
            y = y + skip_row * xconv[p, at, :].astype(F32)
            gate = silu(zs[p, at, :].astype(F32))
            y_ref[p, at, :] = y * gate
            g_ref[p, at, :] = dot(ef_ref[at, :], matrix) * gate

    def finish(p):
        for i in range(1, 4):
            to_member(p, i).wait_recv()
        carried = c_recv[p].reshape(STATE, WIDE)
        for c in range(subs):
            at = slice(c * SUB, (c + 1) * SUB)
            gated = y_ref[p, at, :] + g_ref[p, at, :] * dot(c_ref[at, :], carried)
            y_ref[p, at, :] = gated
            square = gated * gated
            sq_ref[at, :] += square[:, :128] + square[:, 128:]

    def first_pass(p, carry):
        states(p)
        for i in range(1, 4):
            to_quad(p, i).start()
        q_recv[p, member] = l_send[p, member]

        @pl.when(p == 0)
        def _():
            def wait_decay(i, c):
                source = ((quad + QUADS - i) % QUADS) * 4
                pltpu.make_async_remote_copy(
                    decay_all.at[pl.ds(source, 4)],
                    decay_all.at[pl.ds(source, 4)],
                    d_send2.at[i],
                    d_recv2.at[i],
                    device_id={"slot": far_peer(i)},
                    device_id_type=MESH,
                ).wait_recv()
                return c

            lax.fori_loop(1, QUADS, wait_decay, 0)
            for k in range(slots):
                decay_rows[k : k + 1, :] = decay_all[k]
            rest = decay_rows[...]
            wide = [jnp.zeros((slots, WIDE), F32) for _ in range(PARTS)]
            for _ in range(3):
                term = rest.astype(BF16)
                rest = rest - term.astype(F32)
                for q in range(PARTS):
                    r = iota((128, WIDE), 0)
                    matrix = (r == 4 * q + iota((128, WIDE), 1) // HEAD_DIM).astype(F32).astype(BF16)
                    wide[q] = wide[q] + dot(term, matrix)
            for q in range(PARTS):
                decay_wide[2 * q] = wide[q][:, :128]
                decay_wide[2 * q + 1] = wide[q][:, 128:]

        @pl.when(p >= 1)
        def _():
            quad_totals(p - 1)

        @pl.when((p >= 2) & (my_part == p - 2))
        def _():
            own()

        return carry

    def second_pass(p, carry):
        @pl.when(p == 0)
        def _():
            quad_totals(PARTS - 1)

        @pl.when((p < 2) & (my_part == p + 2))
        def _():
            own()

        local(p)

        @pl.when(p >= 1)
        def _():
            members(p - 1)

        return carry

    lax.fori_loop(0, PARTS, first_pass, 0)
    lax.fori_loop(0, PARTS, second_pass, 0)
    members(PARTS - 1)
    sq_ref[...] = jnp.zeros_like(sq_ref)
    lax.fori_loop(0, PARTS, lambda p, c: (finish(p), c)[1], 0)

    sums = exact_dot(jnp.ones((8, 128), F32), sq_ref[...], ((1,), (1,)))
    n_send[0] = sums[0:1]
    n_recv[tp] = sums[0:1]

    def to_tp(i):
        return pltpu.make_async_remote_copy(
            n_send.at[0],
            n_recv.at[tp],
            ns.at[i],
            nr.at[i],
            device_id={"tp": (tp + i) % tp_size},
            device_id_type=MESH,
        )

    for i in range(1, tp_size):
        to_tp(i).start()
    for i in range(1, tp_size):
        to_tp(i).wait_recv()
    n_rows[...] = jnp.zeros_like(n_rows)
    for k in range(tp_size):
        n_rows[k : k + 1, :] = n_recv[k]
    everyone = exact_dot(n_rows[...], jnp.ones((8, 128), F32), ((0,), (0,)))
    sq_ref[...] = lax.rsqrt(everyone * (1.0 / (PARTS * WIDE * tp_size)) + EPSILON)

    def out_copy(p):
        return pltpu.make_async_copy(
            o_ref.at[p], out_hbm.at[:, pl.ds(p * WIDE, WIDE)], out_sem.at[p]
        )

    def write(p, carry):
        gain = norm_ref[p]
        for c in range(subs):
            at = slice(c * SUB, (c + 1) * SUB)
            scale = sq_ref[at, :]
            scale = jnp.concatenate([scale, scale], axis=1)
            o_ref[p, at, :] = (y_ref[p, at, :] * scale * gain).astype(BF16)
        return carry

    for p in range(PARTS):
        write(p, 0)
        out_copy(p).start()

    for halo in halos:
        halo.wait_send()
    for i in range(1, 4):
        near_decay(i).wait_send()
    lax.fori_loop(1, QUADS, lambda i, c: (far_decay(i).wait_send(), c)[1], 0)
    for p in range(PARTS):
        for i in range(1, 4):
            to_quad(p, i).wait_send()
            to_member(p, i).wait_send()
        for tile in range(4):

            @pl.when(owner_of(p, tile) != quad)
            def _():
                to_owner(p, tile).wait_send()

    lax.fori_loop(1, QUADS, lambda i, c: (from_owner(i).wait_send(), c)[1], 0)
    for i in range(1, tp_size):
        to_tp(i).wait_send()
    for p in range(PARTS):
        out_copy(p).wait()


def body(x_in, bc_in, z_gate, decay_rate, step_size, d_skip, conv_x, conv_bc, norm_weight, lengths):
    tokens, columns = x_in.shape
    subs = tokens // SUB
    tp_size = lax.axis_size("tp")
    heads = columns // HEAD_DIM
    vmem = pl.BlockSpec(memory_space=pltpu.VMEM)
    hbm = pl.BlockSpec(memory_space=pl.ANY)
    dma = pltpu.SemaphoreType.DMA
    split_taps = conv_x.reshape(4, PARTS, WIDE).transpose(1, 0, 2)
    return pl.pallas_call(
        functools.partial(kernel, tp_size),
        out_shape=jax.ShapeDtypeStruct((tokens, columns), BF16),
        in_specs=[pl.BlockSpec(memory_space=pltpu.SMEM), hbm, vmem, hbm] + [vmem] * 6,
        out_specs=hbm,
        scratch_shapes=[
            pltpu.VMEM((PARTS, 16 + tokens, WIDE), BF16),
            pltpu.VMEM((PARTS, tokens, WIDE), BF16),
            pltpu.VMEM((16 + tokens, 2 * STATE), BF16),
            pltpu.VMEM((subs, 3 * SUB, 80), BF16),
            pltpu.VMEM((subs, SUB, STATE + SUB), BF16),
            pltpu.VMEM((PARTS, subs, STATE + SUB, WIDE), BF16),
            pltpu.VMEM((subs, STATE, SUB), BF16),
            pltpu.VMEM((tokens, STATE), BF16),
            pltpu.VMEM((PARTS, tokens, WIDE), BF16),
            pltpu.VMEM((tokens, 32), F32),
            pltpu.VMEM((16, 32), F32),
            pltpu.VMEM((16, 32), F32),
            pltpu.VMEM((tokens, 32), BF16),
            pltpu.VMEM((tokens, 32), BF16),
            pltpu.VMEM((tokens, 32), BF16),
            pltpu.VMEM((64, 32), BF16),
            pltpu.VMEM((PARTS, tokens, WIDE), F32),
            pltpu.VMEM((PARTS, tokens, WIDE), F32),
            pltpu.VMEM((tokens, 128), F32),
            pltpu.VMEM((PARTS, tokens, WIDE), BF16),
            pltpu.VMEM((4 * QUADS, 1, 128), F32),
            pltpu.VMEM((4 * QUADS, 128), F32),
            pltpu.VMEM((8, 4 * QUADS, 128), F32),
            pltpu.VMEM((PARTS, 4, 32, WIDE), BF16),
            pltpu.VMEM((PARTS, 4, 32, WIDE), BF16),
            pltpu.VMEM((PARTS, 4, 16, 128), BF16),
            pltpu.VMEM((QUADS, 16, 128), BF16),
            pltpu.VMEM((QUADS, 16, 128), BF16),
            pltpu.VMEM((PARTS, 4, 16, 128), BF16),
            pltpu.VMEM((PARTS, 4, 32, WIDE), BF16),
            pltpu.VMEM((PARTS, 4, 32, WIDE), BF16),
            pltpu.VMEM((1, 1, tokens), F32),
            pltpu.VMEM((tp_size, 1, tokens), F32),
            pltpu.VMEM((8, tokens), F32),
            dma((2 * PARTS,)),
            dma((PARTS,)),
            dma((PARTS + 1,)),
            dma((PARTS + 1,)),
            dma((4,)),
            dma((4,)),
            dma((QUADS,)),
            dma((QUADS,)),
            dma((PARTS, 4)),
            dma((PARTS, 4)),
            dma((PARTS, 4)),
            dma((QUADS,)),
            dma((QUADS,)),
            dma((PARTS, 4)),
            dma((PARTS, 4)),
            dma((PARTS, 4)),
            dma((tp_size,)),
            dma((tp_size,)),
        ],
        compiler_params=pltpu.CompilerParams(
            collective_id=0, has_side_effects=True, vmem_limit_bytes=56 * 1024 * 1024
        ),
    )(
        lengths,
        x_in,
        bc_in,
        z_gate,
        decay_rate,
        step_size,
        d_skip.reshape(1, heads),
        split_taps,
        conv_bc,
        norm_weight.reshape(PARTS, 1, WIDE),
    )


def solution(mesh):
    placed = (
        P("slot", "tp"),
        P("slot", "tp"),
        P("slot", "tp"),
        P("slot", "tp"),
        P("slot", "tp"),
        P("tp"),
        P(None, "tp"),
        P(None, "tp"),
        P("tp"),
        P(),
    )
    return jax.shard_map(
        body, mesh=mesh, in_specs=placed, out_specs=P("slot", "tp"), check_vma=False
    )
```

```python
import functools

import jax
import jax.numpy as jnp
from jax import lax
from jax.experimental import pallas as pl
from jax.experimental.pallas import tpu as pltpu
from jax.sharding import PartitionSpec as P

MESH = pl.DeviceIdType.MESH
HEAD_DIM = 64
STATE = 128
SUB = 64
PARTS = 4
WIDE = 256
QUADS = 16
EPSILON = 1e-05
F32 = jnp.float32
BF16 = jnp.bfloat16


def silu(v):
    half = 0.5 * v
    return half * jnp.tanh(half) + half


def dot(a, b):
    return jnp.dot(a, b, preferred_element_type=F32)


def exact_dot(a, b, dims):
    return lax.dot_general(
        a, b, (dims, ((), ())), precision=lax.Precision.HIGHEST, preferred_element_type=F32
    )


def iota(shape, axis):
    return lax.broadcasted_iota(jnp.int32, shape, axis)


def two_terms(v):
    high = v.astype(BF16).astype(F32)
    return jnp.where(iota(v.shape, 1) < 16, high, v - high).astype(BF16)


def kernel(
    tp_size,
    len_ref,
    x_hbm,
    bc_ref,
    z_hbm,
    rate_ref,
    step_ref,
    skip_ref,
    conv_x_ref,
    conv_bc_ref,
    y_ref,
    sq_ref,
    xs,
    zs,
    x_edge,
    bc_edge,
    bc0_ref,
    bcs,
    shift_ref,
    group_ref,
    left_ref,
    right_ref,
    c_ref,
    xconv,
    cum_ref,
    st_ref,
    u_ref,
    e_send,
    e_recv,
    e_rows,
    n_state,
    mid_ref,
    end_ref,
    f_ref,
    e_ref,
    ef_ref,
    rows_ref,
    g_ref,
    decay_all,
    decay_rows,
    decay_wide,
    decay_near,
    l_send,
    q_recv,
    t_send,
    o_recv,
    o_send,
    g_recv,
    p_send,
    c_recv,
    n_send,
    n_recv,
    in_sem,
    halo_send,
    halo_recv,
    edge_send,
    edge_recv,
    d_send1,
    d_recv1,
    d_send2,
    d_recv2,
    s1,
    r1,
    s2,
    r2,
    s3,
    r3,
    s4,
    r4,
    ns,
    nr,
):
    tokens = x_hbm.shape[0]
    subs = tokens // SUB
    slots = 4 * QUADS
    slot = lax.axis_index("slot")
    tp = lax.axis_index("tp")
    quad = slot // 4
    member = slot % 4
    first_row = slot * tokens
    after, before = (slot + 1) % slots, (slot + slots - 1) % slots

    def quad_peer(i):
        return quad * 4 + (member + i) % 4

    def far_peer(i):
        return ((quad + i) % QUADS) * 4 + member

    def x_copy(p):
        return pltpu.make_async_copy(
            x_hbm.at[:, pl.ds(p * WIDE, WIDE)], xs.at[p, pl.ds(16, tokens)], in_sem.at[p]
        )

    def z_copy(p):
        return pltpu.make_async_copy(
            z_hbm.at[:, pl.ds(p * WIDE, WIDE)], zs.at[p], in_sem.at[PARTS + p]
        )

    barrier = pltpu.get_barrier_semaphore()

    def greet(peer):
        pl.semaphore_signal(barrier, inc=1, device_id={"slot": peer}, device_id_type=MESH)

    lax.fori_loop(1, QUADS, lambda i, c: (greet(far_peer(i)), c)[1], 0)
    for i in range(1, 4):
        greet(quad_peer(i))
    greet(after)
    greet(before)
    for i in range(1, tp_size):
        pl.semaphore_signal(
            barrier, inc=1, device_id={"tp": (tp + i) % tp_size}, device_id_type=MESH
        )
    for p in range(PARTS):
        x_copy(p).start()
    for p in range(PARTS):
        z_copy(p).start()

    ends = []
    total = 0
    for i in range(4):
        total = total + len_ref[i]
        ends.append(total)

    def start_of(pos, bounds):
        start = jnp.zeros_like(pos)
        for end in bounds:
            start = jnp.where(pos >= end, end, start)
        return start

    zero_one = iota((128, 128), 0), iota((128, 128), 1)
    tri = ((zero_one[0] >= zero_one[1]) & (zero_one[0] // SUB == zero_one[1] // SUB)).astype(F32)
    width = min(128, tokens)
    eye = (zero_one[0] == zero_one[1]).astype(F32)
    for b in range(tokens // width):
        at = slice(b * width, (b + 1) * width)
        rate, step = rate_ref[:, at], step_ref[:, at]
        rate = jnp.concatenate([rate, rate], axis=0)
        step = jnp.concatenate([step, step], axis=0)
        cum_ref[at, :] = exact_dot(tri[:width, :width], rate, ((1,), (1,)))
        st_ref[at, :] = exact_dot(eye[:width, :width], step, ((1,), (1,)))
    mid_ref[...] = jnp.zeros_like(mid_ref)
    end_ref[...] = jnp.zeros_like(end_ref)
    offset = jnp.zeros((1, 32), F32)
    for c in range(subs):
        at = slice(c * SUB, (c + 1) * SUB)
        cum = cum_ref[at, :]
        mid = cum_ref[c * SUB + 31 : c * SUB + 32, :]
        end = cum_ref[c * SUB + 63 : c * SUB + 64, :]
        mid_ref[c : c + 1, :] = mid
        end_ref[c : c + 1, :] = end
        f_ref[at, :] = two_terms(jnp.exp(cum - mid) * st_ref[at, :])
        e_ref[at, :] = two_terms(jnp.exp(mid - cum))
        pos = first_row + c * SUB + iota((SUB, 32), 0)
        open_rows = start_of(pos, ends[:3]) < first_row
        ef_ref[at, :] = two_terms(jnp.where(open_rows, jnp.exp(-(offset + cum)), 0.0))
        offset = offset + end
    last_pos = first_row + tokens - 1 + jnp.zeros((1, 32), jnp.int32)
    whole = start_of(last_pos, ends[:3]) < first_row
    decay = jnp.where(whole, jnp.exp(-offset), 0.0)
    decay_all[slot] = jnp.zeros((1, 128), F32)
    decay_all[slot, :, 0:32] = jnp.where(iota((1, 32), 1) < 16, decay, 0.0)
    g1 = jnp.exp(-mid_ref[...])
    g2 = jnp.exp(mid_ref[...] - end_ref[...])
    sub_pos = first_row + iota((16, 32), 0) * SUB
    keep = start_of(sub_pos + (SUB - 1), ends) < sub_pos
    rows_ref[0:16, :] = two_terms(g1)
    rows_ref[16:32, :] = two_terms(g2)
    rows_ref[32:48, :] = two_terms(jnp.where(keep, g2, 0.0))
    skip = skip_ref[...]
    rows_ref[48:64, :] = two_terms(
        jnp.broadcast_to(jnp.concatenate([skip, skip], axis=1), (16, 32))
    )

    blocks = [(row, min(192, tokens - row)) for row in range(0, tokens, 192)]

    def shifts_at(row, count):
        t = iota((count, count + 16), 0)
        s = iota((count, count + 16), 1) - 16
        inside = (first_row + row + s) >= start_of(first_row + row + t, ends)
        return [((s == t - d) & inside).astype(F32).astype(BF16) for d in range(1, 4)]

    for k, (row, count) in enumerate(blocks):
        for d, one in enumerate(shifts_at(row, count)):
            shift_ref[k, d * count : (d + 1) * count, : count + 16] = one

    bcs[:16, :] = jnp.zeros((16, 2 * STATE), BF16)
    bcs[16:, :] = bc_ref[...]
    for p in range(PARTS):
        xs[p, :16, :] = jnp.zeros((16, WIDE), BF16)

    def conv(rows, shifts, taps):
        moved = dot(shifts, rows)
        count = rows.shape[0] - 16
        summed = taps[3:4] * rows[16:].astype(F32)
        for d in range(1, 4):
            summed = summed + taps[3 - d : 4 - d] * moved[(d - 1) * count : d * count]
        return silu(summed).astype(BF16)

    def block_shifts(k):
        count = blocks[k][1]
        return shift_ref[k, : 3 * count, : count + 16]

    groups = [(c, min(4, subs - c)) for c in range(0, subs, 4)]

    def keys_and_queries(c, bc, again=False):
        base = first_row + c * SUB
        key, query = bc[:, :STATE], bc[:, STATE:]
        c_ref[c * SUB : (c + 1) * SUB, :] = query
        if c == 0:
            bc0_ref[...] = bc
        scores = lax.dot_general(query, key, (((1,), (1,)), ((), ())), preferred_element_type=F32)
        t = iota((SUB, SUB), 0)
        s = iota((SUB, SUB), 1)
        seen = (t >= s) & ((base + s) >= start_of(base + t, ends))
        left_ref[c, :, STATE:] = jnp.where(seen, scores, 0.0).astype(BF16)
        row = base + iota((SUB, STATE), 0)
        from_before = start_of(row, ends) < base
        left_ref[c, :, :STATE] = jnp.where(from_before, query.astype(F32), 0.0).astype(BF16)
        last = start_of(jnp.zeros((SUB, STATE), jnp.int32) + (base + SUB - 1), ends)
        keys = jnp.where(row >= last, key.astype(F32), 0.0)
        if not again:
            g, i = c // 4, c % 4
            group_ref[g, i * STATE : (i + 1) * STATE, i * SUB : (i + 1) * SUB] = keys.T.astype(BF16)

    group_ref[...] = jnp.zeros_like(group_ref)
    for k, (row, count) in enumerate(blocks):
        bc = conv(bcs[row : row + count + 16, :], block_shifts(k), conv_bc_ref[...])
        for i in range(count // SUB):
            keys_and_queries(row // SUB + i, bc[i * SUB : (i + 1) * SUB])

    def widen_matrix(p, rows):
        r = iota((rows, WIDE), 0) % 16
        return (r == 4 * p + iota((rows, WIDE), 1) // HEAD_DIM).astype(F32).astype(BF16)

    def row_factors(p):
        return dot(rows_ref[...], widen_matrix(p, 32))

    def later_subs(p, carry):
        x_copy(p).wait()
        taps = conv_x_ref[p]
        wide_f = dot(f_ref[...], widen_matrix(p, 32))
        rows = row_factors(p)
        parts = []
        for k, (row, count) in enumerate(blocks):
            values = conv(xs[p, row : row + count + 16, :], block_shifts(k), taps)
            xconv[p, row : row + count, :] = values
            scaled = values.astype(F32) * wide_f[row : row + count]
            if row == 0:
                scaled = jnp.where(iota(scaled.shape, 0) >= 3, scaled, 0.0)
            scaled = scaled.astype(BF16)
            for i in range(count // SUB):
                one = scaled[i * SUB : (i + 1) * SUB]
                right_ref[p, row // SUB + i, STATE:, :] = one
                parts.append(one)
        state = jnp.zeros((STATE, WIDE), F32)
        for g, (first, many) in enumerate(groups):
            scaled = jnp.concatenate(parts[first : first + many], axis=0)
            adds = dot(group_ref[g, : many * STATE, : many * SUB], scaled)
            for i in range(many):
                c = first + i
                add = adds[i * STATE : (i + 1) * STATE]
                u_ref[p, c] = add
                if c == 0:
                    state = rows[16:17] * add
                else:
                    state = rows[32 + c : 33 + c] * rows[c : c + 1] * state + rows[16 + c : 17 + c] * add
        l_send[p] = state.astype(BF16).reshape(4, 32, WIDE)
        q_recv[p, member] = l_send[p, member]
        return carry

    def edge_fade(rows):
        fade = rows[16:17]
        for c in range(1, subs):
            fade = fade * rows[32 + c : 33 + c] * rows[c : c + 1]
        return fade

    edge_shape = (16, STATE)

    def edge():
        shifts = jnp.concatenate(shifts_at(0, 16), axis=0)
        halos[PARTS].wait_recv()
        bc = conv(bc_edge[...], shifts, conv_bc_ref[...])
        bc0_ref[0:16, :] = bc
        row = first_row + iota(edge_shape, 0)
        last = start_of(jnp.zeros(edge_shape, jnp.int32) + (first_row + SUB - 1), ends)
        keys = jnp.where(row >= last, bc[:, :STATE].astype(F32), 0.0)
        for t in range(3):
            e_send[t, :, PARTS * WIDE :] = keys[t : t + 1]
        for p in range(PARTS):
            halos[p].wait_recv()
        every = range(PARTS)
        rows = [row_factors(p) for p in every]
        wide_f = [dot(f_ref[0:16, :], widen_matrix(p, 32)) for p in every]
        values = [conv(x_edge[p], shifts, conv_x_ref[p]) for p in every]
        scaled = [(values[p].astype(F32) * wide_f[p]).astype(BF16) for p in every]
        for p in every:
            faded = scaled[p].astype(F32) * edge_fade(rows[p])
            for t in range(3):
                e_send[t, :, p * WIDE : (p + 1) * WIDE] = faded[t : t + 1]
        for i in range(1, 4):
            edge_to(i).start()
        first_three = jnp.where(iota(edge_shape, 0) < 3, keys, 0.0).astype(BF16)
        for p in every:
            xconv[p, 0:16, :] = values[p]
            right_ref[p, 0, STATE : STATE + 16, :] = scaled[p]
            u_ref[p, 0] += lax.dot_general(
                first_three, scaled[p], (((0,), (0,)), ((), ())), preferred_element_type=F32
            )
        keys_and_queries(0, bc0_ref[...], again=True)

    def edge_to(i):
        return pltpu.make_async_remote_copy(
            e_send,
            e_recv.at[pl.ds(member * 3, 3)],
            edge_send.at[i],
            edge_recv.at[i],
            device_id={"slot": quad_peer(i)},
            device_id_type=MESH,
        )

    def edge_rows():
        for i in range(1, 4):
            edge_to(i).wait_recv()
        for t in range(3):
            e_recv[member * 3 + t] = e_send[t]
        e_rows[...] = jnp.zeros_like(e_rows)
        for i in range(4):
            for t in range(3):
                e_rows[i, t : t + 1, :] = e_recv[i * 3 + t]

    def quad_state(p, i):
        pick = (iota((32, STATE), 1) == member * 32 + iota((32, STATE), 0)).astype(F32).astype(BF16)
        keys = e_rows[i, :, PARTS * WIDE :].astype(BF16)
        keys = lax.dot_general(pick, keys, (((1,), (1,)), ((), ())), preferred_element_type=F32)
        values = e_rows[i, :, p * WIDE : (p + 1) * WIDE].astype(BF16)
        return q_recv[p, i].astype(F32) + dot(keys.astype(BF16), values)

    def chain(p):
        rows = row_factors(p)
        right_ref[p, 0, :STATE, :] = jnp.zeros((STATE, WIDE), BF16)
        state = rows[16:17] * u_ref[p, 0]
        for c in range(1, subs):
            faded = rows[c : c + 1] * state
            right_ref[p, c, :STATE, :] = faded.astype(BF16)
            if c + 1 < subs:
                state = rows[32 + c : 33 + c] * faded + rows[16 + c : 17 + c] * u_ref[p, c]

    lax.fori_loop(0, PARTS, later_subs, 0)
    for p in range(PARTS):
        x_edge[p, 16:, :] = xs[p, 16:32, :]
    bc_edge[16:, :] = bc_ref[:16, :]

    def to_quad(p, i):
        return pltpu.make_async_remote_copy(
            l_send.at[p, (member + i) % 4],
            q_recv.at[p, member],
            s1.at[p, i],
            r1.at[p, i],
            device_id={"slot": quad_peer(i)},
            device_id_type=MESH,
        )

    pl.semaphore_wait(barrier, 2 + 3 + (QUADS - 1) + (tp_size - 1))
    halos = []
    for p in range(PARTS):
        halos.append(
            pltpu.make_async_remote_copy(
                x_hbm.at[pl.ds(tokens - 16, 16), pl.ds(p * WIDE, WIDE)],
                x_edge.at[p, pl.ds(0, 16)],
                halo_send.at[p],
                halo_recv.at[p],
                device_id={"slot": after},
                device_id_type=MESH,
            )
        )
    halos.append(
        pltpu.make_async_remote_copy(
            bc_ref.at[pl.ds(tokens - 16, 16)],
            bc_edge.at[pl.ds(0, 16)],
            halo_send.at[PARTS],
            halo_recv.at[PARTS],
            device_id={"slot": after},
            device_id_type=MESH,
        )
    )
    halos[PARTS].start()
    for p in range(PARTS):
        halos[p].start()

    def near_decay(i):
        return pltpu.make_async_remote_copy(
            decay_all.at[slot],
            decay_all.at[slot],
            d_send1.at[i],
            d_recv1.at[i],
            device_id={"slot": quad_peer(i)},
            device_id_type=MESH,
        )

    def far_decay(i):
        return pltpu.make_async_remote_copy(
            decay_all.at[pl.ds(quad * 4, 4)],
            decay_all.at[pl.ds(quad * 4, 4)],
            d_send2.at[i],
            d_recv2.at[i],
            device_id={"slot": far_peer(i)},
            device_id_type=MESH,
        )

    for p in range(PARTS):
        for i in range(1, 4):
            to_quad(p, i).start()
    for i in range(1, 4):
        near_decay(i).start()


    def owner_of(p, tile):
        return 4 * tile + (p + 4 - tile) % 4

    def to_owner(p, tile):
        return pltpu.make_async_remote_copy(
            t_send.at[p, tile],
            o_recv.at[quad],
            s2.at[p, tile],
            r2.at[quad],
            device_id={"slot": owner_of(p, tile) * 4 + member},
            device_id_type=MESH,
        )

    my_part = (quad // 4 + quad % 4) % 4
    my_tile = quad // 4

    def from_owner(i):
        return pltpu.make_async_remote_copy(
            o_send.at[(quad + i) % QUADS],
            g_recv.at[my_part, my_tile],
            s3.at[i],
            r3.at[my_part, my_tile],
            device_id={"slot": far_peer(i)},
            device_id_type=MESH,
        )

    def to_member(p, i):
        return pltpu.make_async_remote_copy(
            p_send.at[p, (member + i) % 4],
            c_recv.at[p, member],
            s4.at[p, i],
            r4.at[p, i],
            device_id={"slot": quad_peer(i)},
            device_id_type=MESH,
        )

    def decay_of(p, i):
        return decay_near[p, i : i + 1, :]

    def quad_totals(p):
        for i in range(1, 4):
            to_quad(p, i).wait_recv()
        run = quad_state(p, 0)
        n_state[p, 0] = run
        for i in range(1, 4):
            new = quad_state(p, i)
            n_state[p, i] = new
            run = decay_of(p, i) * run + new
        run = run.astype(BF16)
        for tile in range(4):
            r, l = tile // 2, tile % 2
            t_send[p, tile] = run[16 * r : 16 * r + 16, 128 * l : 128 * l + 128]
        for tile in range(4):
            mine = owner_of(p, tile) == quad

            @pl.when(mine)
            def _():
                o_recv[quad] = t_send[p, tile]

            @pl.when(jnp.logical_not(mine))
            def _():
                to_owner(p, tile).start()

    def own():
        def wait_one(i, c):
            source = (quad + i) % QUADS
            pltpu.make_async_remote_copy(
                t_send.at[0, 0],
                o_recv.at[source],
                s2.at[0, 0],
                r2.at[source],
                device_id={"slot": far_peer(i)},
                device_id_type=MESH,
            ).wait_recv()
            return c

        lax.fori_loop(1, QUADS, wait_one, 0)
        tile = 2 * my_part + my_tile % 2
        run = jnp.zeros((16, 128), F32)
        for q in range(QUADS):
            o_send[q] = run.astype(BF16)
            fade = decay_wide[tile, 4 * q : 4 * q + 1, :]
            for i in range(1, 4):
                fade = fade * decay_wide[tile, 4 * q + i : 4 * q + i + 1, :]
            run = fade * run + o_recv[q].astype(F32)
        g_recv[my_part, my_tile] = o_send[quad]
        lax.fori_loop(1, QUADS, lambda i, c: (from_owner(i).start(), c)[1], 0)

    def members(p):
        for tile in range(4):

            @pl.when(owner_of(p, tile) != quad)
            def _():
                pltpu.make_async_remote_copy(
                    o_send.at[0],
                    g_recv.at[p, tile],
                    s3.at[0],
                    r3.at[p, tile],
                    device_id={"slot": after},
                    device_id_type=MESH,
                ).wait_recv()

        tiles = [g_recv[p, tile].astype(F32) for tile in range(4)]
        run = jnp.concatenate(
            [
                jnp.concatenate([tiles[0], tiles[1]], axis=1),
                jnp.concatenate([tiles[2], tiles[3]], axis=1),
            ],
            axis=0,
        )
        for i in range(4):
            p_send[p, i] = run.astype(BF16)
            if i < 3:
                run = decay_of(p, i) * run + n_state[p, i]
        c_recv[p, member] = p_send[p, member]
        for i in range(1, 4):
            to_member(p, i).start()

    def local(p):
        z_copy(p).wait()
        matrix = widen_matrix(p, 32)
        skip_row = dot(rows_ref[48:64, :], matrix)[0:1]
        for c in range(subs):
            at = slice(c * SUB, (c + 1) * SUB)
            y = dot(left_ref[c], right_ref[p, c]) * dot(e_ref[at, :], matrix)
            y = y + skip_row * xconv[p, at, :].astype(F32)
            gate = silu(zs[p, at, :].astype(F32))
            y_ref[p, at, :] = y * gate
            g_ref[p, at, :] = dot(ef_ref[at, :], matrix) * gate

    def finish(p):
        for i in range(1, 4):
            to_member(p, i).wait_recv()
        carried = c_recv[p].reshape(STATE, WIDE)
        for c in range(subs):
            at = slice(c * SUB, (c + 1) * SUB)
            gated = y_ref[p, at, :] + g_ref[p, at, :] * dot(c_ref[at, :], carried)
            y_ref[p, at, :] = gated
            square = gated * gated
            sq_ref[at, :] += square[:, :128] + square[:, 128:]

    def second_pass(p, carry):
        chain(p)
        local(p)
        return carry

    edge()
    lax.fori_loop(0, 2, second_pass, 0)
    for i in range(1, 4):
        near_decay(i).wait_recv()
    lax.fori_loop(1, QUADS, lambda i, c: (far_decay(i).start(), c)[1], 0)
    near = jnp.zeros((8, 128), F32)
    for i in range(4):
        near = jnp.where(iota((8, 128), 0) == i, decay_all[quad * 4 + i], near)
    for p in range(PARTS):
        rest = near
        wide = jnp.zeros((8, WIDE), F32)
        r = iota((128, WIDE), 0)
        matrix = (r == 4 * p + iota((128, WIDE), 1) // HEAD_DIM).astype(F32).astype(BF16)
        for _ in range(3):
            term = rest.astype(BF16)
            rest = rest - term.astype(F32)
            wide = wide + dot(term, matrix)
        decay_near[p] = wide
    edge_rows()
    for p in range(PARTS):
        quad_totals(p)
    lax.fori_loop(2, PARTS, second_pass, 0)

    def wait_decay(i, c):
        source = ((quad + QUADS - i) % QUADS) * 4
        pltpu.make_async_remote_copy(
            decay_all.at[pl.ds(source, 4)],
            decay_all.at[pl.ds(source, 4)],
            d_send2.at[i],
            d_recv2.at[i],
            device_id={"slot": far_peer(i)},
            device_id_type=MESH,
        ).wait_recv()
        return c

    lax.fori_loop(1, QUADS, wait_decay, 0)
    for k in range(slots):
        decay_rows[k : k + 1, :] = decay_all[k]
    rest = decay_rows[...]
    wide = [jnp.zeros((slots, WIDE), F32) for _ in range(PARTS)]
    for _ in range(3):
        term = rest.astype(BF16)
        rest = rest - term.astype(F32)
        for q in range(PARTS):
            r = iota((128, WIDE), 0)
            matrix = (r == 4 * q + iota((128, WIDE), 1) // HEAD_DIM).astype(F32).astype(BF16)
            wide[q] = wide[q] + dot(term, matrix)
    for q in range(PARTS):
        decay_wide[2 * q] = wide[q][:, :128]
        decay_wide[2 * q + 1] = wide[q][:, 128:]
    own()
    lax.fori_loop(0, PARTS, lambda p, c: (members(p), c)[1], 0)
    sq_ref[...] = jnp.zeros_like(sq_ref)
    lax.fori_loop(0, PARTS, lambda p, c: (finish(p), c)[1], 0)

    def over_columns(v):
        return lax.dot_general(
            jnp.ones((16, 128), BF16), v, (((1,), (1,)), ((), ())), preferred_element_type=F32
        )

    high = sq_ref[...].astype(BF16)
    low = (sq_ref[...] - high.astype(F32)).astype(BF16)
    sums = over_columns(high) + over_columns(low)
    n_send[0] = sums[0:1]
    n_recv[tp] = sums[0:1]

    def to_tp(i):
        return pltpu.make_async_remote_copy(
            n_send.at[0],
            n_recv.at[tp],
            ns.at[i],
            nr.at[i],
            device_id={"tp": (tp + i) % tp_size},
            device_id_type=MESH,
        )

    for i in range(1, tp_size):
        to_tp(i).start()
    for i in range(1, tp_size):
        to_tp(i).wait_recv()
    everyone = n_recv[0]
    for k in range(1, tp_size):
        everyone = everyone + n_recv[k]
    scale = lax.rsqrt(everyone * (1.0 / (PARTS * WIDE * tp_size)) + EPSILON)
    high = scale.astype(BF16).astype(F32)
    row = iota((16, tokens), 0)
    terms = jnp.where(row == 0, high, jnp.where(row == 1, scale - high, 0.0)).astype(BF16)
    sq_ref[...] = lax.dot_general(
        terms, jnp.ones((16, 128), BF16), (((0,), (0,)), ((), ())), preferred_element_type=F32
    )

    for halo in halos:
        halo.wait_send()
    for i in range(1, 4):
        near_decay(i).wait_send()
        edge_to(i).wait_send()
    lax.fori_loop(1, QUADS, lambda i, c: (far_decay(i).wait_send(), c)[1], 0)
    for p in range(PARTS):
        for i in range(1, 4):
            to_quad(p, i).wait_send()
            to_member(p, i).wait_send()
        for tile in range(4):

            @pl.when(owner_of(p, tile) != quad)
            def _():
                to_owner(p, tile).wait_send()

    lax.fori_loop(1, QUADS, lambda i, c: (from_owner(i).wait_send(), c)[1], 0)
    for i in range(1, tp_size):
        to_tp(i).wait_send()


def write(y_ref, scale_ref, norm_ref, out_hbm, out_ref, sem):
    def copy(i):
        return pltpu.make_async_copy(out_ref.at[i], out_hbm.at[pl.ds(i * 128, 128)], sem.at[i])

    blocks = out_ref.shape[0]
    for i in range(blocks):
        at = slice(i * 128, (i + 1) * 128)
        scale = scale_ref[at, :]
        scale = jnp.concatenate([scale, scale], axis=1)
        for p in range(PARTS):
            out_ref[i, :, p * WIDE : (p + 1) * WIDE] = (y_ref[p, at, :] * scale * norm_ref[p]).astype(BF16)
        copy(i).start()
    for i in range(blocks):
        copy(i).wait()


def body(x_in, bc_in, z_gate, decay_rate, step_size, d_skip, conv_x, conv_bc, norm_weight, lengths):
    tokens, columns = x_in.shape
    subs = tokens // SUB
    tp_size = lax.axis_size("tp")
    heads = columns // HEAD_DIM
    vmem = pl.BlockSpec(memory_space=pltpu.VMEM)
    hbm = pl.BlockSpec(memory_space=pl.ANY)
    dma = pltpu.SemaphoreType.DMA
    split_taps = conv_x.reshape(4, PARTS, WIDE).transpose(1, 0, 2)
    gated, scale = pl.pallas_call(
        functools.partial(kernel, tp_size),
        out_shape=[pltpu.VMEM((PARTS, tokens, WIDE), F32), pltpu.VMEM((tokens, 128), F32)],
        in_specs=[pl.BlockSpec(memory_space=pltpu.SMEM), hbm, vmem, hbm] + [vmem] * 5,
        out_specs=[vmem, vmem],
        scratch_shapes=[
            pltpu.VMEM((PARTS, 16 + tokens, WIDE), BF16),
            pltpu.VMEM((PARTS, tokens, WIDE), BF16),
            pltpu.VMEM((PARTS, 32, WIDE), BF16),
            pltpu.VMEM((32, 2 * STATE), BF16),
            pltpu.VMEM((SUB, 2 * STATE), BF16),
            pltpu.VMEM((16 + tokens, 2 * STATE), BF16),
            pltpu.VMEM((-(-subs // 3), 576, 208), BF16),
            pltpu.VMEM((-(-subs // 4), 4 * STATE, 4 * SUB), BF16),
            pltpu.VMEM((subs, SUB, STATE + SUB), BF16),
            pltpu.VMEM((PARTS, subs, STATE + SUB, WIDE), BF16),
            pltpu.VMEM((tokens, STATE), BF16),
            pltpu.VMEM((PARTS, tokens, WIDE), BF16),
            pltpu.VMEM((tokens, 32), F32),
            pltpu.VMEM((tokens, 32), F32),
            pltpu.VMEM((PARTS, subs, STATE, WIDE), F32),
            pltpu.VMEM((3, 1, PARTS * WIDE + STATE), F32),
            pltpu.VMEM((12, 1, PARTS * WIDE + STATE), F32),
            pltpu.VMEM((4, 8, PARTS * WIDE + STATE), F32),
            pltpu.VMEM((PARTS, 4, 32, WIDE), F32),
            pltpu.VMEM((16, 32), F32),
            pltpu.VMEM((16, 32), F32),
            pltpu.VMEM((tokens, 32), BF16),
            pltpu.VMEM((tokens, 32), BF16),
            pltpu.VMEM((tokens, 32), BF16),
            pltpu.VMEM((64, 32), BF16),
            pltpu.VMEM((PARTS, tokens, WIDE), F32),
            pltpu.VMEM((4 * QUADS, 1, 128), F32),
            pltpu.VMEM((4 * QUADS, 128), F32),
            pltpu.VMEM((8, 4 * QUADS, 128), F32),
            pltpu.VMEM((PARTS, 8, WIDE), F32),
            pltpu.VMEM((PARTS, 4, 32, WIDE), BF16),
            pltpu.VMEM((PARTS, 4, 32, WIDE), BF16),
            pltpu.VMEM((PARTS, 4, 16, 128), BF16),
            pltpu.VMEM((QUADS, 16, 128), BF16),
            pltpu.VMEM((QUADS, 16, 128), BF16),
            pltpu.VMEM((PARTS, 4, 16, 128), BF16),
            pltpu.VMEM((PARTS, 4, 32, WIDE), BF16),
            pltpu.VMEM((PARTS, 4, 32, WIDE), BF16),
            pltpu.VMEM((1, 1, tokens), F32),
            pltpu.VMEM((tp_size, 1, tokens), F32),
            dma((2 * PARTS,)),
            dma((PARTS + 1,)),
            dma((PARTS + 1,)),
            dma((4,)),
            dma((4,)),
            dma((4,)),
            dma((4,)),
            dma((QUADS,)),
            dma((QUADS,)),
            dma((PARTS, 4)),
            dma((PARTS, 4)),
            dma((PARTS, 4)),
            dma((QUADS,)),
            dma((QUADS,)),
            dma((PARTS, 4)),
            dma((PARTS, 4)),
            dma((PARTS, 4)),
            dma((tp_size,)),
            dma((tp_size,)),
        ],
        compiler_params=pltpu.CompilerParams(
            collective_id=0, has_side_effects=True, vmem_limit_bytes=56 * 1024 * 1024
        ),
    )(
        lengths,
        x_in,
        bc_in,
        z_gate,
        decay_rate.T,
        step_size.T,
        d_skip.reshape(1, heads),
        split_taps,
        conv_bc,
    )
    return pl.pallas_call(
        write,
        out_shape=jax.ShapeDtypeStruct((tokens, columns), BF16),
        in_specs=[vmem] * 3,
        out_specs=hbm,
        scratch_shapes=[pltpu.VMEM((tokens // 128, 128, columns), BF16), dma((tokens // 128,))],
        compiler_params=pltpu.CompilerParams(vmem_limit_bytes=8 * 1024 * 1024),
    )(gated, scale, norm_weight.reshape(PARTS, 1, WIDE))


def solution(mesh):
    placed = (
        P("slot", "tp"),
        P("slot", "tp"),
        P("slot", "tp"),
        P("slot", "tp"),
        P("slot", "tp"),
        P("tp"),
        P(None, "tp"),
        P(None, "tp"),
        P("tp"),
        P(),
    )
    return jax.shard_map(
        body, mesh=mesh, in_specs=placed, out_specs=P("slot", "tp"), check_vma=False
    )
```

```python
import functools

import jax
import jax.numpy as jnp
from jax import lax
from jax.experimental import pallas as pl
from jax.experimental.pallas import tpu as pltpu
from jax.sharding import PartitionSpec as P

MESH = pl.DeviceIdType.MESH
HEAD_DIM = 64
STATE = 128
SUB = 64
PARTS = 4
WIDE = 256
QUADS = 16
EPSILON = 1e-05
F32 = jnp.float32
BF16 = jnp.bfloat16


def silu(v):
    half = 0.5 * v
    return half * jnp.tanh(half) + half


def dot(a, b):
    return jnp.dot(a, b, preferred_element_type=F32)


def exact_dot(a, b, dims):
    return lax.dot_general(
        a, b, (dims, ((), ())), precision=lax.Precision.HIGHEST, preferred_element_type=F32
    )


def iota(shape, axis):
    return lax.broadcasted_iota(jnp.int32, shape, axis)


def two_terms(v):
    high = v.astype(BF16).astype(F32)
    return jnp.where(iota(v.shape, 1) < 16, high, v - high).astype(BF16)


def kernel(
    tp_size,
    len_hbm,
    x_hbm,
    bc_hbm,
    z_hbm,
    rate_hbm,
    step_hbm,
    skip_hbm,
    conv_x_hbm,
    conv_bc_hbm,
    y_ref,
    sq_ref,
    len_ref,
    rate_ref,
    step_ref,
    skip_ref,
    conv_x_ref,
    conv_bc_ref,
    xs,
    zs,
    x_edge,
    bc_edge,
    bcs,
    shift_ref,
    group_ref,
    left_ref,
    right_ref,
    c_ref,
    xconv,
    cum_ref,
    st_ref,
    u_ref,
    e_send,
    e_recv,
    e_rows,
    n_state,
    mid_ref,
    end_ref,
    f_ref,
    e_ref,
    ef_ref,
    g_all,
    keys_all,
    keys_t,
    rows_ref,
    g_ref,
    decay_all,
    decay_rows,
    decay_wide,
    decay_near,
    l_send,
    q_recv,
    t_send,
    o_recv,
    o_send,
    g_recv,
    p_send,
    c_recv,
    n_send,
    n_recv,
    in_sem,
    halo_send,
    halo_recv,
    edge_send,
    edge_recv,
    d_send1,
    d_recv1,
    d_send2,
    d_recv2,
    s1,
    r1,
    s2,
    r2,
    s3,
    r3,
    s4,
    r4,
    ns,
    nr,
):
    tokens = x_hbm.shape[0]
    subs = tokens // SUB
    slots = 4 * QUADS
    slot = lax.axis_index("slot")
    tp = lax.axis_index("tp")
    quad = slot // 4
    member = slot % 4
    first_row = slot * tokens
    after, before = (slot + 1) % slots, (slot + slots - 1) % slots

    def quad_peer(i):
        return quad * 4 + (member + i) % 4

    owners = [(p, r) for p in range(PARTS) for r in range(2)]
    is_owner = quad % 2 == 1
    my_part = quad // 4
    my_half = (quad % 4) // 2

    def owner_quad(p, r):
        return 4 * p + 1 + 2 * r

    def same_place(q):
        return 4 * q + member

    def x_copy(p):
        return pltpu.make_async_copy(
            x_hbm.at[:, pl.ds(p * WIDE, WIDE)], xs.at[p, pl.ds(16, tokens)], in_sem.at[p]
        )

    def z_copy(p):
        return pltpu.make_async_copy(
            z_hbm.at[:, pl.ds(p * WIDE, WIDE)], zs.at[p], in_sem.at[PARTS + p]
        )

    barrier = pltpu.get_barrier_semaphore()

    small = [
        pltpu.make_async_copy(source, target, in_sem.at[2 * PARTS + k])
        for k, (source, target) in enumerate(
            [
                (rate_hbm, rate_ref),
                (step_hbm, step_ref),
                (len_hbm, len_ref),
                (skip_hbm, skip_ref),
                (bc_hbm, bcs.at[pl.ds(16, tokens)]),
                (conv_bc_hbm, conv_bc_ref),
                (conv_x_hbm, conv_x_ref),
            ]
        )
    ]
    for copy in small:
        copy.start()
    for p in range(PARTS):
        x_copy(p).start()

    def greet(peer):
        pl.semaphore_signal(barrier, inc=1, device_id={"slot": peer}, device_id_type=MESH)

    for p, r in owners:

        @pl.when(quad != owner_quad(p, r))
        def _():
            greet(same_place(owner_quad(p, r)))

    @pl.when(is_owner)
    def _():
        for q in range(0, QUADS, 2):
            greet(same_place(q))

    for i in range(1, 4):
        greet(quad_peer(i))
    greet(after)
    greet(before)
    for i in range(1, tp_size):
        pl.semaphore_signal(
            barrier, inc=1, device_id={"tp": (tp + i) % tp_size}, device_id_type=MESH
        )
    for copy in small[:4]:
        copy.wait()

    ends = []
    total = 0
    for i in range(4):
        total = total + len_ref[i]
        ends.append(total)

    def start_of(pos, bounds):
        start = jnp.zeros_like(pos)
        for end in bounds:
            start = jnp.where(pos >= end, end, start)
        return start

    zero_one = iota((128, 128), 0), iota((128, 128), 1)
    tri = ((zero_one[0] >= zero_one[1]) & (zero_one[0] // SUB == zero_one[1] // SUB)).astype(F32)
    width = min(128, tokens)
    eye = (zero_one[0] == zero_one[1]).astype(F32)
    for b in range(tokens // width):
        at = slice(b * width, (b + 1) * width)
        rate, step = rate_ref[:, at], step_ref[:, at]
        rate = jnp.concatenate([rate, rate], axis=0)
        step = jnp.concatenate([step, step], axis=0)
        cum_ref[at, :] = exact_dot(tri[:width, :width], rate, ((1,), (1,)))
        st_ref[at, :] = exact_dot(eye[:width, :width], step, ((1,), (1,)))
    mid_ref[...] = jnp.zeros_like(mid_ref)
    end_ref[...] = jnp.zeros_like(end_ref)
    offset = jnp.zeros((1, 32), F32)
    for c in range(subs):
        at = slice(c * SUB, (c + 1) * SUB)
        cum = cum_ref[at, :]
        mid = cum_ref[c * SUB + 31 : c * SUB + 32, :]
        end = cum_ref[c * SUB + 63 : c * SUB + 64, :]
        mid_ref[c : c + 1, :] = mid
        end_ref[c : c + 1, :] = end
        f_ref[at, :] = two_terms(jnp.exp(cum - mid) * st_ref[at, :])
        e_ref[at, :] = two_terms(jnp.exp(mid - cum))
        pos = first_row + c * SUB + iota((SUB, 32), 0)
        open_rows = start_of(pos, ends[:3]) < first_row
        ef_ref[at, :] = two_terms(jnp.where(open_rows, jnp.exp(-(offset + cum)), 0.0))
        offset = offset + end
    left_over = jnp.zeros((1, 32), F32)
    last_start = start_of(jnp.zeros((SUB, 32), jnp.int32) + (first_row + tokens - 1), ends)
    for c in reversed(range(subs)):
        at = slice(c * SUB, (c + 1) * SUB)
        end = end_ref[c : c + 1, :]
        pos = first_row + c * SUB + iota((SUB, 32), 0)
        fade = jnp.exp(-(left_over + (end - cum_ref[at, :]))) * st_ref[at, :]
        g_all[at, :] = two_terms(jnp.where(pos >= last_start, fade, 0.0))
        left_over = left_over + end
    last_pos = first_row + tokens - 1 + jnp.zeros((1, 32), jnp.int32)
    whole = start_of(last_pos, ends[:3]) < first_row
    decay = jnp.where(whole, jnp.exp(-offset), 0.0)
    decay_all[slot] = jnp.zeros((1, 128), F32)
    decay_all[slot, :, 0:32] = jnp.where(iota((1, 32), 1) < 16, decay, 0.0)
    g1 = jnp.exp(-mid_ref[...])
    g2 = jnp.exp(mid_ref[...] - end_ref[...])
    sub_pos = first_row + iota((16, 32), 0) * SUB
    keep = start_of(sub_pos + (SUB - 1), ends) < sub_pos
    rows_ref[0:16, :] = two_terms(g1)
    rows_ref[16:32, :] = two_terms(g2)
    rows_ref[32:48, :] = two_terms(jnp.where(keep, g2, 0.0))
    skip = skip_ref[...]
    rows_ref[48:64, :] = two_terms(
        jnp.broadcast_to(jnp.concatenate([skip, skip], axis=1), (16, 32))
    )

    blocks = [(row, min(192, tokens - row)) for row in range(0, tokens, 192)]

    def shifts_at(row, count):
        t = iota((count, count + 16), 0)
        s = iota((count, count + 16), 1) - 16
        inside = (first_row + row + s) >= start_of(first_row + row + t, ends)
        return [((s == t - d) & inside).astype(F32).astype(BF16) for d in range(1, 4)]

    for k, (row, count) in enumerate(blocks):
        for d, one in enumerate(shifts_at(row, count)):
            shift_ref[k, d * count : (d + 1) * count, : count + 16] = one

    bcs[:16, :] = jnp.zeros((16, 2 * STATE), BF16)
    small[4].wait()
    small[5].wait()
    small[6].wait()
    for p in range(PARTS):
        xs[p, :16, :] = jnp.zeros((16, WIDE), BF16)

    def conv(rows, shifts, taps):
        moved = dot(shifts, rows)
        count = rows.shape[0] - 16
        summed = taps[3:4] * rows[16:].astype(F32)
        for d in range(1, 4):
            summed = summed + taps[3 - d : 4 - d] * moved[(d - 1) * count : d * count]
        return silu(summed).astype(BF16)

    def block_shifts(k):
        count = blocks[k][1]
        return shift_ref[k, : 3 * count, : count + 16]

    groups = [(c, min(4, subs - c)) for c in range(0, subs, 4)]

    def keys_and_queries(c):
        base = first_row + c * SUB
        at = slice(c * SUB, (c + 1) * SUB)
        key, query = keys_all[at, :], c_ref[at, :]
        scores = lax.dot_general(query, key, (((1,), (1,)), ((), ())), preferred_element_type=F32)
        t = iota((SUB, SUB), 0)
        s = iota((SUB, SUB), 1)
        seen = (t >= s) & ((base + s) >= start_of(base + t, ends))
        left_ref[c, :, STATE:] = jnp.where(seen, scores, 0.0).astype(BF16)
        row = base + iota((SUB, STATE), 0)
        from_before = start_of(row, ends) < base
        left_ref[c, :, :STATE] = jnp.where(from_before, query.astype(F32), 0.0).astype(BF16)
        last = start_of(jnp.zeros((SUB, STATE), jnp.int32) + (base + SUB - 1), ends)
        keys = jnp.where(row >= last, key.astype(F32), 0.0)
        g, i = c // 4, c % 4
        group_ref[g, i * STATE : (i + 1) * STATE, i * SUB : (i + 1) * SUB] = keys.T.astype(BF16)

    for k, (row, count) in enumerate(blocks):
        bc = conv(bcs[row : row + count + 16, :], block_shifts(k), conv_bc_ref[...])
        keys_all[row : row + count, :] = bc[:, :STATE]
        c_ref[row : row + count, :] = bc[:, STATE:]
    for b in range(tokens // width):
        at = slice(b * width, (b + 1) * width)
        keys_t[:, at] = keys_all[at, :].astype(F32).T.astype(BF16)

    def widen_matrix(p, rows):
        r = iota((rows, WIDE), 0) % 16
        return (r == 4 * p + iota((rows, WIDE), 1) // HEAD_DIM).astype(F32).astype(BF16)

    def row_factors(p):
        return dot(rows_ref[...], widen_matrix(p, 32))

    def later_subs(p):
        taps = conv_x_ref[p]
        wide_g = dot(g_all[...], widen_matrix(p, 32))
        parts = []
        for k, (row, count) in enumerate(blocks):
            values = conv(xs[p, row : row + count + 16, :], block_shifts(k), taps)
            xconv[p, row : row + count, :] = values
            scaled = values.astype(F32) * wide_g[row : row + count]
            if row == 0:
                scaled = jnp.where(iota(scaled.shape, 0) >= 3, scaled, 0.0)
            parts.append(scaled.astype(BF16))
        state = dot(keys_t[...], jnp.concatenate(parts, axis=0))
        l_send[p] = state.astype(BF16).reshape(4, 32, WIDE)
        q_recv[p, member] = l_send[p, member]

    def add_subs(p):
        wide_f = dot(f_ref[...], widen_matrix(p, 32))
        for g, (first, many) in enumerate(groups):
            at = slice(first * SUB, (first + many) * SUB)
            scaled = (xconv[p, at, :].astype(F32) * wide_f[at]).astype(BF16)
            adds = dot(group_ref[g, : many * STATE, : many * SUB], scaled)
            for i in range(many):
                right_ref[p, first + i, STATE:, :] = scaled[i * SUB : (i + 1) * SUB]
                u_ref[p, first + i] = adds[i * STATE : (i + 1) * STATE]

    def edge():
        shifts = jnp.concatenate(shifts_at(0, 16), axis=0)
        halos[PARTS].wait_recv()
        bc = conv(bc_edge[...], shifts, conv_bc_ref[...])
        keys_all[0:16, :] = bc[:, :STATE]
        c_ref[0:16, :] = bc[:, STATE:]
        keys = bc[:, :STATE].astype(F32)
        for t in range(3):
            e_send[t, :, PARTS * WIDE :] = keys[t : t + 1]
        for p in range(PARTS):
            halos[p].wait_recv()
        every = range(PARTS)
        wide_g = [dot(g_all[0:16, :], widen_matrix(p, 32)) for p in every]
        values = [conv(x_edge[p], shifts, conv_x_ref[p]) for p in every]
        for p in every:
            faded = values[p].astype(F32) * wide_g[p]
            for t in range(3):
                e_send[t, :, p * WIDE : (p + 1) * WIDE] = faded[t : t + 1]
        for i in range(1, 4):
            edge_to(i).start()
        for p in every:
            xconv[p, 0:16, :] = values[p]
        group_ref[...] = jnp.zeros_like(group_ref)
        for c in range(subs):
            keys_and_queries(c)

    def edge_to(i):
        return pltpu.make_async_remote_copy(
            e_send,
            e_recv.at[pl.ds(member * 3, 3)],
            edge_send.at[i],
            edge_recv.at[i],
            device_id={"slot": quad_peer(i)},
            device_id_type=MESH,
        )

    def edge_rows():
        for i in range(1, 4):
            edge_to(i).wait_recv()
        for t in range(3):
            e_recv[member * 3 + t] = e_send[t]
        e_rows[...] = jnp.zeros_like(e_rows)
        for i in range(4):
            for t in range(3):
                e_rows[i, t : t + 1, :] = e_recv[i * 3 + t]

    def quad_state(p, i):
        pick = (iota((32, STATE), 1) == member * 32 + iota((32, STATE), 0)).astype(F32).astype(BF16)
        keys = e_rows[i, :, PARTS * WIDE :].astype(BF16)
        keys = lax.dot_general(pick, keys, (((1,), (1,)), ((), ())), preferred_element_type=F32)
        values = e_rows[i, :, p * WIDE : (p + 1) * WIDE].astype(BF16)
        return q_recv[p, i].astype(F32) + dot(keys.astype(BF16), values)

    def chain(p):
        rows = row_factors(p)
        right_ref[p, 0, :STATE, :] = jnp.zeros((STATE, WIDE), BF16)
        state = rows[16:17] * u_ref[p, 0]
        for c in range(1, subs):
            faded = rows[c : c + 1] * state
            right_ref[p, c, :STATE, :] = faded.astype(BF16)
            if c + 1 < subs:
                state = rows[32 + c : 33 + c] * faded + rows[16 + c : 17 + c] * u_ref[p, c]

    for p in range(PARTS):
        x_copy(p).wait()
    for p in range(PARTS):
        later_subs(p)
    for p in range(PARTS):
        x_edge[p, 16:, :] = xs[p, 16:32, :]
    bc_edge[16:, :] = bcs[16:32, :]
    for p in range(PARTS):
        z_copy(p).start()

    def to_quad(p, i):
        return pltpu.make_async_remote_copy(
            l_send.at[p, (member + i) % 4],
            q_recv.at[p, member],
            s1.at[p, i],
            r1.at[p, i],
            device_id={"slot": quad_peer(i)},
            device_id_type=MESH,
        )

    pl.semaphore_wait(barrier, 2 + 3 + (tp_size - 1) + jnp.where(is_owner, QUADS - 1, len(owners)))
    halos = []
    for p in range(PARTS):
        halos.append(
            pltpu.make_async_remote_copy(
                x_hbm.at[pl.ds(tokens - 16, 16), pl.ds(p * WIDE, WIDE)],
                x_edge.at[p, pl.ds(0, 16)],
                halo_send.at[p],
                halo_recv.at[p],
                device_id={"slot": after},
                device_id_type=MESH,
            )
        )
    halos.append(
        pltpu.make_async_remote_copy(
            bc_hbm.at[pl.ds(tokens - 16, 16)],
            bc_edge.at[pl.ds(0, 16)],
            halo_send.at[PARTS],
            halo_recv.at[PARTS],
            device_id={"slot": after},
            device_id_type=MESH,
        )
    )
    halos[PARTS].start()
    for p in range(PARTS):
        halos[p].start()

    def near_decay(i):
        return pltpu.make_async_remote_copy(
            decay_all.at[slot],
            decay_all.at[slot],
            d_send1.at[i],
            d_recv1.at[i],
            device_id={"slot": quad_peer(i)},
            device_id_type=MESH,
        )

    def far_decay(p, r):
        return pltpu.make_async_remote_copy(
            decay_all.at[pl.ds(quad * 4, 4)],
            decay_all.at[pl.ds(quad * 4, 4)],
            d_send2.at[2 * p + r],
            d_recv2.at[quad],
            device_id={"slot": same_place(owner_quad(p, r))},
            device_id_type=MESH,
        )

    def each_far_owner(act):
        for p, r in owners:

            @pl.when(quad != owner_quad(p, r))
            def _():
                act(p, r)

    for p in range(PARTS):
        for i in range(1, 4):
            to_quad(p, i).start()
    for i in range(1, 4):
        near_decay(i).start()


    def to_owner(p, r):
        return pltpu.make_async_remote_copy(
            t_send.at[p, r],
            o_recv.at[quad],
            s2.at[p, r],
            r2.at[quad],
            device_id={"slot": same_place(owner_quad(p, r))},
            device_id_type=MESH,
        )

    def from_owner(q):
        return pltpu.make_async_remote_copy(
            o_send.at[q],
            g_recv.at[my_part, my_half],
            s3.at[q],
            r3.at[my_part, my_half],
            device_id={"slot": same_place(q)},
            device_id_type=MESH,
        )

    def to_member(p, i):
        return pltpu.make_async_remote_copy(
            p_send.at[p, (member + i) % 4],
            c_recv.at[p, member],
            s4.at[p, i],
            r4.at[p, i],
            device_id={"slot": quad_peer(i)},
            device_id_type=MESH,
        )

    def decay_of(p, i):
        return decay_near[p, i : i + 1, :]

    def quad_totals(p):
        for i in range(1, 4):
            to_quad(p, i).wait_recv()
        run = quad_state(p, 0)
        n_state[p, 0] = run
        for i in range(1, 4):
            new = quad_state(p, i)
            n_state[p, i] = new
            run = decay_of(p, i) * run + new
        run = run.astype(BF16)
        for r in range(2):
            t_send[p, r] = run[16 * r : 16 * r + 16]
            mine = owner_quad(p, r) == quad

            @pl.when(mine)
            def _():
                o_recv[quad] = t_send[p, r]

            @pl.when(jnp.logical_not(mine))
            def _():
                to_owner(p, r).start()

    def own():
        run = jnp.zeros((16, WIDE), F32)
        for q in range(QUADS):
            o_send[q] = run.astype(BF16)
            other = quad != q

            @pl.when(other)
            def _():
                from_owner(q).start()
                to_owner_of(q).wait_recv()

            fade = decay_wide[4 * q : 4 * q + 1, :]
            for i in range(1, 4):
                fade = fade * decay_wide[4 * q + i : 4 * q + i + 1, :]
            run = fade * run + o_recv[q].astype(F32)
        g_recv[my_part, my_half] = o_send[quad]

    def to_owner_of(q):
        return pltpu.make_async_remote_copy(
            t_send.at[0, 0],
            o_recv.at[q],
            s2.at[0, 0],
            r2.at[q],
            device_id={"slot": same_place(q)},
            device_id_type=MESH,
        )

    def members(p):
        for r in range(2):

            @pl.when(owner_quad(p, r) != quad)
            def _():
                pltpu.make_async_remote_copy(
                    o_send.at[0],
                    g_recv.at[p, r],
                    s3.at[0],
                    r3.at[p, r],
                    device_id={"slot": after},
                    device_id_type=MESH,
                ).wait_recv()

        run = g_recv[p].reshape(32, WIDE).astype(F32)
        for i in range(4):
            p_send[p, i] = run.astype(BF16)
            if i < 3:
                run = decay_of(p, i) * run + n_state[p, i]
        c_recv[p, member] = p_send[p, member]
        for i in range(1, 4):
            to_member(p, i).start()

    def local(p):
        z_copy(p).wait()
        matrix = widen_matrix(p, 32)
        skip_row = dot(rows_ref[48:64, :], matrix)[0:1]
        for c in range(subs):
            at = slice(c * SUB, (c + 1) * SUB)
            y = dot(left_ref[c], right_ref[p, c]) * dot(e_ref[at, :], matrix)
            y = y + skip_row * xconv[p, at, :].astype(F32)
            gate = silu(zs[p, at, :].astype(F32))
            y_ref[p, at, :] = y * gate
            g_ref[p, at, :] = dot(ef_ref[at, :], matrix) * gate

    def finish(p):
        for i in range(1, 4):
            to_member(p, i).wait_recv()
        carried = c_recv[p].reshape(STATE, WIDE)
        for c in range(subs):
            at = slice(c * SUB, (c + 1) * SUB)
            gated = y_ref[p, at, :] + g_ref[p, at, :] * dot(c_ref[at, :], carried)
            y_ref[p, at, :] = gated
            square = gated * gated
            sq_ref[at, :] += square[:, :128] + square[:, 128:]

    def second_pass(p, carry):
        add_subs(p)
        chain(p)
        local(p)
        return carry

    edge()
    lax.fori_loop(0, 2, second_pass, 0)
    for i in range(1, 4):
        near_decay(i).wait_recv()
    each_far_owner(lambda p, r: far_decay(p, r).start())
    near = jnp.zeros((8, 128), F32)
    for i in range(4):
        near = jnp.where(iota((8, 128), 0) == i, decay_all[quad * 4 + i], near)
    for p in range(PARTS):
        rest = near
        wide = jnp.zeros((8, WIDE), F32)
        r = iota((128, WIDE), 0)
        matrix = (r == 4 * p + iota((128, WIDE), 1) // HEAD_DIM).astype(F32).astype(BF16)
        for _ in range(3):
            term = rest.astype(BF16)
            rest = rest - term.astype(F32)
            wide = wide + dot(term, matrix)
        decay_near[p] = wide
    edge_rows()
    for p in range(PARTS):
        quad_totals(p)
    lax.fori_loop(2, PARTS, second_pass, 0)

    for halo in halos:
        halo.wait_send()
    for i in range(1, 4):
        near_decay(i).wait_send()
        edge_to(i).wait_send()
        for p in range(PARTS):
            to_quad(p, i).wait_send()
    each_far_owner(lambda p, r: far_decay(p, r).wait_send())

    @pl.when(is_owner)
    def _():
        for q in range(QUADS):

            @pl.when(quad != q)
            def _():
                pltpu.make_async_remote_copy(
                    decay_all.at[pl.ds(4 * q, 4)],
                    decay_all.at[pl.ds(4 * q, 4)],
                    d_send2.at[0],
                    d_recv2.at[q],
                    device_id={"slot": same_place(q)},
                    device_id_type=MESH,
                ).wait_recv()

        for k in range(slots):
            decay_rows[k : k + 1, :] = decay_all[k]
        rest = decay_rows[...]
        wide = jnp.zeros((slots, WIDE), F32)
        r = iota((128, WIDE), 0)
        matrix = (r == 4 * my_part + iota((128, WIDE), 1) // HEAD_DIM).astype(F32).astype(BF16)
        for _ in range(3):
            term = rest.astype(BF16)
            rest = rest - term.astype(F32)
            wide = wide + dot(term, matrix)
        decay_wide[...] = wide
        own()

    each_far_owner(lambda p, r: to_owner(p, r).wait_send())
    lax.fori_loop(0, PARTS, lambda p, c: (members(p), c)[1], 0)

    @pl.when(is_owner)
    def _():
        lax.fori_loop(1, QUADS, lambda i, c: (from_owner((quad + i) % QUADS).wait_send(), c)[1], 0)

    sq_ref[...] = jnp.zeros_like(sq_ref)
    lax.fori_loop(0, PARTS, lambda p, c: (finish(p), c)[1], 0)

    def over_columns(v):
        return lax.dot_general(
            jnp.ones((16, 128), BF16), v, (((1,), (1,)), ((), ())), preferred_element_type=F32
        )

    high = sq_ref[...].astype(BF16)
    low = (sq_ref[...] - high.astype(F32)).astype(BF16)
    sums = over_columns(high) + over_columns(low)
    n_send[0] = sums[0:1]
    n_recv[tp] = sums[0:1]

    def to_tp(i):
        return pltpu.make_async_remote_copy(
            n_send.at[0],
            n_recv.at[tp],
            ns.at[i],
            nr.at[i],
            device_id={"tp": (tp + i) % tp_size},
            device_id_type=MESH,
        )

    for i in range(1, tp_size):
        to_tp(i).start()
    for p in range(PARTS):
        for i in range(1, 4):
            to_member(p, i).wait_send()
    for i in range(1, tp_size):
        to_tp(i).wait_recv()
    everyone = n_recv[0]
    for k in range(1, tp_size):
        everyone = everyone + n_recv[k]
    scale = lax.rsqrt(everyone * (1.0 / (PARTS * WIDE * tp_size)) + EPSILON)
    high = scale.astype(BF16).astype(F32)
    row = iota((16, tokens), 0)
    terms = jnp.where(row == 0, high, jnp.where(row == 1, scale - high, 0.0)).astype(BF16)
    sq_ref[...] = lax.dot_general(
        terms, jnp.ones((16, 128), BF16), (((0,), (0,)), ((), ())), preferred_element_type=F32
    )

    for i in range(1, tp_size):
        to_tp(i).wait_send()


def write(y_ref, scale_ref, norm_ref, out_hbm, out_ref, sem):
    def copy(i):
        return pltpu.make_async_copy(out_ref.at[i], out_hbm.at[pl.ds(i * 128, 128)], sem.at[i])

    blocks = out_ref.shape[0]
    for i in range(blocks):
        at = slice(i * 128, (i + 1) * 128)
        scale = scale_ref[at, :]
        scale = jnp.concatenate([scale, scale], axis=1)
        for p in range(PARTS):
            out_ref[i, :, p * WIDE : (p + 1) * WIDE] = (y_ref[p, at, :] * scale * norm_ref[p]).astype(BF16)
        copy(i).start()
    for i in range(blocks):
        copy(i).wait()


def body(x_in, bc_in, z_gate, decay_rate, step_size, d_skip, conv_x, conv_bc, norm_weight, lengths):
    tokens, columns = x_in.shape
    subs = tokens // SUB
    tp_size = lax.axis_size("tp")
    heads = columns // HEAD_DIM
    vmem = pl.BlockSpec(memory_space=pltpu.VMEM)
    hbm = pl.BlockSpec(memory_space=pl.ANY)
    dma = pltpu.SemaphoreType.DMA
    split_taps = conv_x.reshape(4, PARTS, WIDE).transpose(1, 0, 2)
    gated, scale = pl.pallas_call(
        functools.partial(kernel, tp_size),
        out_shape=[pltpu.VMEM((PARTS, tokens, WIDE), F32), pltpu.VMEM((tokens, 128), F32)],
        in_specs=[hbm] * 9,
        out_specs=[vmem, vmem],
        scratch_shapes=[
            pltpu.SMEM((4,), jnp.int32),
            pltpu.VMEM((heads, tokens), F32),
            pltpu.VMEM((heads, tokens), F32),
            pltpu.VMEM((1, heads), F32),
            pltpu.VMEM((PARTS, 4, WIDE), F32),
            pltpu.VMEM((4, 2 * STATE), F32),
            pltpu.VMEM((PARTS, 16 + tokens, WIDE), BF16),
            pltpu.VMEM((PARTS, tokens, WIDE), BF16),
            pltpu.VMEM((PARTS, 32, WIDE), BF16),
            pltpu.VMEM((32, 2 * STATE), BF16),
            pltpu.VMEM((16 + tokens, 2 * STATE), BF16),
            pltpu.VMEM((-(-subs // 3), 576, 208), BF16),
            pltpu.VMEM((-(-subs // 4), 4 * STATE, 4 * SUB), BF16),
            pltpu.VMEM((subs, SUB, STATE + SUB), BF16),
            pltpu.VMEM((PARTS, subs, STATE + SUB, WIDE), BF16),
            pltpu.VMEM((tokens, STATE), BF16),
            pltpu.VMEM((PARTS, tokens, WIDE), BF16),
            pltpu.VMEM((tokens, 32), F32),
            pltpu.VMEM((tokens, 32), F32),
            pltpu.VMEM((PARTS, subs, STATE, WIDE), F32),
            pltpu.VMEM((3, 1, PARTS * WIDE + STATE), F32),
            pltpu.VMEM((12, 1, PARTS * WIDE + STATE), F32),
            pltpu.VMEM((4, 8, PARTS * WIDE + STATE), F32),
            pltpu.VMEM((PARTS, 4, 32, WIDE), F32),
            pltpu.VMEM((16, 32), F32),
            pltpu.VMEM((16, 32), F32),
            pltpu.VMEM((tokens, 32), BF16),
            pltpu.VMEM((tokens, 32), BF16),
            pltpu.VMEM((tokens, 32), BF16),
            pltpu.VMEM((tokens, 32), BF16),
            pltpu.VMEM((tokens, STATE), BF16),
            pltpu.VMEM((STATE, tokens), BF16),
            pltpu.VMEM((64, 32), BF16),
            pltpu.VMEM((PARTS, tokens, WIDE), F32),
            pltpu.VMEM((4 * QUADS, 1, 128), F32),
            pltpu.VMEM((4 * QUADS, 128), F32),
            pltpu.VMEM((4 * QUADS, WIDE), F32),
            pltpu.VMEM((PARTS, 8, WIDE), F32),
            pltpu.VMEM((PARTS, 4, 32, WIDE), BF16),
            pltpu.VMEM((PARTS, 4, 32, WIDE), BF16),
            pltpu.VMEM((PARTS, 2, 16, WIDE), BF16),
            pltpu.VMEM((QUADS, 16, WIDE), BF16),
            pltpu.VMEM((QUADS, 16, WIDE), BF16),
            pltpu.VMEM((PARTS, 2, 16, WIDE), BF16),
            pltpu.VMEM((PARTS, 4, 32, WIDE), BF16),
            pltpu.VMEM((PARTS, 4, 32, WIDE), BF16),
            pltpu.VMEM((1, 1, tokens), F32),
            pltpu.VMEM((tp_size, 1, tokens), F32),
            dma((2 * PARTS + 7,)),
            dma((PARTS + 1,)),
            dma((PARTS + 1,)),
            dma((4,)),
            dma((4,)),
            dma((4,)),
            dma((4,)),
            dma((QUADS,)),
            dma((QUADS,)),
            dma((PARTS, 4)),
            dma((PARTS, 4)),
            dma((PARTS, 4)),
            dma((QUADS,)),
            dma((QUADS,)),
            dma((PARTS, 4)),
            dma((PARTS, 4)),
            dma((PARTS, 4)),
            dma((tp_size,)),
            dma((tp_size,)),
        ],
        compiler_params=pltpu.CompilerParams(
            collective_id=0, has_side_effects=True, vmem_limit_bytes=56 * 1024 * 1024
        ),
    )(
        lengths,
        x_in,
        bc_in,
        z_gate,
        decay_rate.T,
        step_size.T,
        d_skip.reshape(1, heads),
        split_taps,
        conv_bc,
    )
    return pl.pallas_call(
        write,
        out_shape=jax.ShapeDtypeStruct((tokens, columns), BF16),
        in_specs=[vmem] * 3,
        out_specs=hbm,
        scratch_shapes=[pltpu.VMEM((tokens // 128, 128, columns), BF16), dma((tokens // 128,))],
        compiler_params=pltpu.CompilerParams(vmem_limit_bytes=8 * 1024 * 1024),
    )(gated, scale, norm_weight.reshape(PARTS, 1, WIDE))


def solution(mesh):
    placed = (
        P("slot", "tp"),
        P("slot", "tp"),
        P("slot", "tp"),
        P("slot", "tp"),
        P("slot", "tp"),
        P("tp"),
        P(None, "tp"),
        P(None, "tp"),
        P("tp"),
        P(),
    )
    return jax.shard_map(
        body, mesh=mesh, in_specs=placed, out_specs=P("slot", "tp"), check_vma=False
    )
```

```python
import functools

import jax
import jax.numpy as jnp
from jax import lax
from jax.experimental import pallas as pl
from jax.experimental.pallas import tpu as pltpu
from jax.sharding import PartitionSpec as P

MESH = pl.DeviceIdType.MESH
HEAD_DIM = 64
STATE = 128
SUB = 64
PARTS = 4
WIDE = 256
QUADS = 16
EPSILON = 1e-05
F32 = jnp.float32
BF16 = jnp.bfloat16


def silu(v):
    half = 0.5 * v
    return half * jnp.tanh(half) + half


def dot(a, b):
    return jnp.dot(a, b, preferred_element_type=F32)


def exact_dot(a, b, dims):
    return lax.dot_general(
        a, b, (dims, ((), ())), precision=lax.Precision.HIGHEST, preferred_element_type=F32
    )


def iota(shape, axis):
    return lax.broadcasted_iota(jnp.int32, shape, axis)


def two_terms(v):
    high = v.astype(BF16).astype(F32)
    return jnp.where(iota(v.shape, 1) < 16, high, v - high).astype(BF16)


def kernel(
    tp_size,
    len_hbm,
    x_hbm,
    bc_hbm,
    z_hbm,
    rate_hbm,
    step_hbm,
    skip_hbm,
    conv_x_hbm,
    conv_bc_hbm,
    y_ref,
    sq_ref,
    len_ref,
    rate_ref,
    step_ref,
    skip_ref,
    conv_x_ref,
    conv_bc_ref,
    xs,
    zs,
    x_edge,
    bc_edge,
    bcs,
    shift_ref,
    group_ref,
    left_ref,
    right_ref,
    c_ref,
    xconv,
    cum_ref,
    st_ref,
    u_ref,
    e_send,
    e_recv,
    e_rows,
    n_state,
    mid_ref,
    end_ref,
    f_ref,
    e_ref,
    ef_ref,
    g_all,
    keys_all,
    keys_t,
    rows_ref,
    g_ref,
    decay_all,
    decay_rows,
    decay_wide,
    decay_near,
    l_send,
    q_recv,
    t_send,
    o_recv,
    o_send,
    g_recv,
    p_send,
    c_recv,
    n_send,
    n_recv,
    in_sem,
    halo_send,
    halo_recv,
    edge_send,
    edge_recv,
    d_send1,
    d_recv1,
    d_send2,
    d_recv2,
    s1,
    r1,
    s2,
    r2,
    s3,
    r3,
    s4,
    r4,
    ns,
    nr,
):
    tokens = x_hbm.shape[0]
    subs = tokens // SUB
    slots = 4 * QUADS
    slot = lax.axis_index("slot")
    tp = lax.axis_index("tp")
    quad = slot // 4
    member = slot % 4
    first_row = slot * tokens
    after, before = (slot + 1) % slots, (slot + slots - 1) % slots

    def quad_peer(i):
        return quad * 4 + (member + i) % 4

    owners = [(p, r) for p in range(PARTS) for r in range(2)]
    is_owner = quad % 2 == 1
    my_part = quad // 4
    my_half = (quad % 4) // 2

    def owner_quad(p, r):
        return 4 * p + 1 + 2 * r

    def same_place(q):
        return 4 * q + member

    def x_copy(p):
        return pltpu.make_async_copy(
            x_hbm.at[:, pl.ds(p * WIDE, WIDE)], xs.at[p, pl.ds(16, tokens)], in_sem.at[p]
        )

    def z_copy(p):
        return pltpu.make_async_copy(
            z_hbm.at[:, pl.ds(p * WIDE, WIDE)], zs.at[p], in_sem.at[PARTS + p]
        )

    barrier = pltpu.get_barrier_semaphore()

    small = [
        pltpu.make_async_copy(source, target, in_sem.at[2 * PARTS + k])
        for k, (source, target) in enumerate(
            [
                (rate_hbm, rate_ref),
                (step_hbm, step_ref),
                (len_hbm, len_ref),
                (skip_hbm, skip_ref),
                (bc_hbm, bcs.at[pl.ds(16, tokens)]),
                (conv_bc_hbm, conv_bc_ref),
                (conv_x_hbm, conv_x_ref),
            ]
        )
    ]
    for copy in small:
        copy.start()
    for p in range(PARTS):
        x_copy(p).start()

    def greet(peer):
        pl.semaphore_signal(barrier, inc=1, device_id={"slot": peer}, device_id_type=MESH)

    for p, r in owners:

        @pl.when(quad != owner_quad(p, r))
        def _():
            greet(same_place(owner_quad(p, r)))

    @pl.when(is_owner)
    def _():
        for q in range(0, QUADS, 2):
            greet(same_place(q))

    for i in range(1, 4):
        greet(quad_peer(i))
    greet(after)
    greet(before)
    for i in range(1, tp_size):
        pl.semaphore_signal(
            barrier, inc=1, device_id={"tp": (tp + i) % tp_size}, device_id_type=MESH
        )
    for copy in small[:4]:
        copy.wait()

    ends = []
    total = 0
    for i in range(4):
        total = total + len_ref[i]
        ends.append(total)

    def start_of(pos, bounds):
        start = jnp.zeros_like(pos)
        for end in bounds:
            start = jnp.where(pos >= end, end, start)
        return start

    zero_one = iota((128, 128), 0), iota((128, 128), 1)
    tri = ((zero_one[0] >= zero_one[1]) & (zero_one[0] // SUB == zero_one[1] // SUB)).astype(F32)
    width = min(128, tokens)
    eye = (zero_one[0] == zero_one[1]).astype(F32)
    for b in range(tokens // width):
        at = slice(b * width, (b + 1) * width)
        rate, step = rate_ref[:, at], step_ref[:, at]
        rate = jnp.concatenate([rate, rate], axis=0)
        step = jnp.concatenate([step, step], axis=0)
        cum_ref[at, :] = exact_dot(tri[:width, :width], rate, ((1,), (1,)))
        st_ref[at, :] = exact_dot(eye[:width, :width], step, ((1,), (1,)))
    mid_ref[...] = jnp.zeros_like(mid_ref)
    end_ref[...] = jnp.zeros_like(end_ref)
    offset = jnp.zeros((1, 32), F32)
    for c in range(subs):
        at = slice(c * SUB, (c + 1) * SUB)
        cum = cum_ref[at, :]
        mid = cum_ref[c * SUB + 31 : c * SUB + 32, :]
        end = cum_ref[c * SUB + 63 : c * SUB + 64, :]
        mid_ref[c : c + 1, :] = mid
        end_ref[c : c + 1, :] = end
        f_ref[at, :] = two_terms(jnp.exp(cum - mid) * st_ref[at, :])
        e_ref[at, :] = two_terms(jnp.exp(mid - cum))
        pos = first_row + c * SUB + iota((SUB, 32), 0)
        open_rows = start_of(pos, ends[:3]) < first_row
        ef_ref[at, :] = two_terms(jnp.where(open_rows, jnp.exp(-(offset + cum)), 0.0))
        offset = offset + end
    left_over = jnp.zeros((1, 32), F32)
    last_start = start_of(jnp.zeros((SUB, 32), jnp.int32) + (first_row + tokens - 1), ends)
    for c in reversed(range(subs)):
        at = slice(c * SUB, (c + 1) * SUB)
        end = end_ref[c : c + 1, :]
        pos = first_row + c * SUB + iota((SUB, 32), 0)
        fade = jnp.exp(-(left_over + (end - cum_ref[at, :]))) * st_ref[at, :]
        g_all[at, :] = two_terms(jnp.where(pos >= last_start, fade, 0.0))
        left_over = left_over + end
    last_pos = first_row + tokens - 1 + jnp.zeros((1, 32), jnp.int32)
    whole = start_of(last_pos, ends[:3]) < first_row
    decay = jnp.where(whole, jnp.exp(-offset), 0.0)
    decay_all[slot] = jnp.zeros((1, 128), F32)
    decay_all[slot, :, 0:32] = jnp.where(iota((1, 32), 1) < 16, decay, 0.0)
    g1 = jnp.exp(-mid_ref[...])
    g2 = jnp.exp(mid_ref[...] - end_ref[...])
    sub_pos = first_row + iota((16, 32), 0) * SUB
    keep = start_of(sub_pos + (SUB - 1), ends) < sub_pos
    rows_ref[0:16, :] = two_terms(g1)
    rows_ref[16:32, :] = two_terms(g2)
    rows_ref[32:48, :] = two_terms(jnp.where(keep, g2, 0.0))
    skip = skip_ref[...]
    rows_ref[48:64, :] = two_terms(
        jnp.broadcast_to(jnp.concatenate([skip, skip], axis=1), (16, 32))
    )

    blocks = [(row, min(192, tokens - row)) for row in range(0, tokens, 192)]

    def shifts_at(row, count):
        t = iota((count, count + 16), 0)
        s = iota((count, count + 16), 1) - 16
        inside = (first_row + row + s) >= start_of(first_row + row + t, ends)
        return [((s == t - d) & inside).astype(F32).astype(BF16) for d in range(1, 4)]

    for k, (row, count) in enumerate(blocks):
        for d, one in enumerate(shifts_at(row, count)):
            shift_ref[k, d * count : (d + 1) * count, : count + 16] = one

    bcs[:16, :] = jnp.zeros((16, 2 * STATE), BF16)
    small[4].wait()
    small[5].wait()
    small[6].wait()
    for p in range(PARTS):
        xs[p, :16, :] = jnp.zeros((16, WIDE), BF16)

    def conv(rows, shifts, taps):
        moved = dot(shifts, rows)
        count = rows.shape[0] - 16
        summed = taps[3:4] * rows[16:].astype(F32)
        for d in range(1, 4):
            summed = summed + taps[3 - d : 4 - d] * moved[(d - 1) * count : d * count]
        return silu(summed).astype(BF16)

    def block_shifts(k):
        count = blocks[k][1]
        return shift_ref[k, : 3 * count, : count + 16]

    groups = [(c, min(4, subs - c)) for c in range(0, subs, 4)]

    def keys_and_queries(c):
        base = first_row + c * SUB
        at = slice(c * SUB, (c + 1) * SUB)
        key, query = keys_all[at, :], c_ref[at, :]
        scores = lax.dot_general(query, key, (((1,), (1,)), ((), ())), preferred_element_type=F32)
        t = iota((SUB, SUB), 0)
        s = iota((SUB, SUB), 1)
        seen = (t >= s) & ((base + s) >= start_of(base + t, ends))
        left_ref[c, :, STATE:] = jnp.where(seen, scores, 0.0).astype(BF16)
        row = base + iota((SUB, STATE), 0)
        from_before = start_of(row, ends) < base
        left_ref[c, :, :STATE] = jnp.where(from_before, query.astype(F32), 0.0).astype(BF16)
        last = start_of(jnp.zeros((SUB, STATE), jnp.int32) + (base + SUB - 1), ends)
        keys = jnp.where(row >= last, key.astype(F32), 0.0)
        g, i = c // 4, c % 4
        group_ref[g, i * STATE : (i + 1) * STATE, i * SUB : (i + 1) * SUB] = keys.T.astype(BF16)

    for k, (row, count) in enumerate(blocks):
        bc = conv(bcs[row : row + count + 16, :], block_shifts(k), conv_bc_ref[...])
        keys_all[row : row + count, :] = bc[:, :STATE]
        c_ref[row : row + count, :] = bc[:, STATE:]
    for b in range(tokens // width):
        at = slice(b * width, (b + 1) * width)
        keys_t[:, at] = keys_all[at, :].astype(F32).T.astype(BF16)

    def widen_matrix(p, rows):
        r = iota((rows, WIDE), 0) % 16
        return (r == 4 * p + iota((rows, WIDE), 1) // HEAD_DIM).astype(F32).astype(BF16)

    def row_factors(p):
        return dot(rows_ref[...], widen_matrix(p, 32))

    def later_subs(p):
        taps = conv_x_ref[p]
        wide_g = dot(g_all[...], widen_matrix(p, 32))
        parts = []
        for k, (row, count) in enumerate(blocks):
            values = conv(xs[p, row : row + count + 16, :], block_shifts(k), taps)
            xconv[p, row : row + count, :] = values
            scaled = values.astype(F32) * wide_g[row : row + count]
            if row == 0:
                scaled = jnp.where(iota(scaled.shape, 0) >= 3, scaled, 0.0)
            parts.append(scaled.astype(BF16))
        state = dot(keys_t[...], jnp.concatenate(parts, axis=0))
        l_send[p] = state.astype(BF16).reshape(4, 32, WIDE)
        q_recv[p, member] = l_send[p, member]

    def add_subs(p):
        wide_f = dot(f_ref[...], widen_matrix(p, 32))
        for g, (first, many) in enumerate(groups):
            at = slice(first * SUB, (first + many) * SUB)
            scaled = (xconv[p, at, :].astype(F32) * wide_f[at]).astype(BF16)
            adds = dot(group_ref[g, : many * STATE, : many * SUB], scaled)
            for i in range(many):
                right_ref[p, first + i, STATE:, :] = scaled[i * SUB : (i + 1) * SUB]
                u_ref[p, first + i] = adds[i * STATE : (i + 1) * STATE]

    def edge():
        shifts = jnp.concatenate(shifts_at(0, 16), axis=0)
        every = range(PARTS)
        wide_g = [dot(g_all[0:16, :], widen_matrix(p, 32)) for p in every]
        for halo in halos:
            halo.wait_recv()
        bc = conv(bc_edge[...], shifts, conv_bc_ref[...])
        keys_all[0:16, :] = bc[:, :STATE]
        c_ref[0:16, :] = bc[:, STATE:]
        keys = bc[:, :STATE].astype(F32)
        for t in range(3):
            e_send[t, :, PARTS * WIDE :] = keys[t : t + 1]
        values = [conv(x_edge[p], shifts, conv_x_ref[p]) for p in every]
        for p in every:
            faded = values[p].astype(F32) * wide_g[p]
            for t in range(3):
                e_send[t, :, p * WIDE : (p + 1) * WIDE] = faded[t : t + 1]
        for i in range(1, 4):
            edge_to(i).start()
        for i in range(1, 4):
            near_decay(i).wait_recv()
        each_far_owner(lambda p, r: far_decay(p, r).start())
        for p in every:
            xconv[p, 0:16, :] = values[p]
        group_ref[...] = jnp.zeros_like(group_ref)
        for c in range(subs):
            keys_and_queries(c)

    def edge_to(i):
        return pltpu.make_async_remote_copy(
            e_send,
            e_recv.at[pl.ds(member * 3, 3)],
            edge_send.at[i],
            edge_recv.at[i],
            device_id={"slot": quad_peer(i)},
            device_id_type=MESH,
        )

    def edge_rows():
        for i in range(1, 4):
            edge_to(i).wait_recv()
        for t in range(3):
            e_recv[member * 3 + t] = e_send[t]
        e_rows[...] = jnp.zeros_like(e_rows)
        for i in range(4):
            for t in range(3):
                e_rows[i, t : t + 1, :] = e_recv[i * 3 + t]

        pick = (iota((32, STATE), 1) == member * 32 + iota((32, STATE), 0)).astype(F32).astype(BF16)
        for i in range(4):
            keys = e_rows[i, :, PARTS * WIDE :].astype(BF16)
            keys = lax.dot_general(pick, keys, (((1,), (1,)), ((), ())), preferred_element_type=F32)
            adds = dot(keys.astype(BF16), e_rows[i, :, : PARTS * WIDE].astype(BF16))
            for p in range(PARTS):
                n_state[p, i] = adds[:, p * WIDE : (p + 1) * WIDE]

    def quad_state(p, i):
        return q_recv[p, i].astype(F32) + n_state[p, i]

    def chain(p):
        rows = row_factors(p)
        right_ref[p, 0, :STATE, :] = jnp.zeros((STATE, WIDE), BF16)
        state = rows[16:17] * u_ref[p, 0]
        for c in range(1, subs):
            faded = rows[c : c + 1] * state
            right_ref[p, c, :STATE, :] = faded.astype(BF16)
            if c + 1 < subs:
                state = rows[32 + c : 33 + c] * faded + rows[16 + c : 17 + c] * u_ref[p, c]

    for p in range(PARTS):
        x_copy(p).wait()
    for p in range(PARTS):
        x_edge[p, 16:, :] = xs[p, 16:32, :]
    bc_edge[16:, :] = bcs[16:32, :]
    for p in range(PARTS):
        z_copy(p).start()

    def to_quad(p, i):
        return pltpu.make_async_remote_copy(
            l_send.at[p, (member + i) % 4],
            q_recv.at[p, member],
            s1.at[p, i],
            r1.at[p, i],
            device_id={"slot": quad_peer(i)},
            device_id_type=MESH,
        )

    pl.semaphore_wait(barrier, 2 + 3 + (tp_size - 1) + jnp.where(is_owner, QUADS - 1, len(owners)))
    halos = []
    for p in range(PARTS):
        halos.append(
            pltpu.make_async_remote_copy(
                x_hbm.at[pl.ds(tokens - 16, 16), pl.ds(p * WIDE, WIDE)],
                x_edge.at[p, pl.ds(0, 16)],
                halo_send.at[p],
                halo_recv.at[p],
                device_id={"slot": after},
                device_id_type=MESH,
            )
        )
    halos.append(
        pltpu.make_async_remote_copy(
            bc_hbm.at[pl.ds(tokens - 16, 16)],
            bc_edge.at[pl.ds(0, 16)],
            halo_send.at[PARTS],
            halo_recv.at[PARTS],
            device_id={"slot": after},
            device_id_type=MESH,
        )
    )
    halos[PARTS].start()
    for p in range(PARTS):
        halos[p].start()

    def near_decay(i):
        return pltpu.make_async_remote_copy(
            decay_all.at[slot],
            decay_all.at[slot],
            d_send1.at[i],
            d_recv1.at[i],
            device_id={"slot": quad_peer(i)},
            device_id_type=MESH,
        )

    def far_decay(p, r):
        return pltpu.make_async_remote_copy(
            decay_all.at[pl.ds(quad * 4, 4)],
            decay_all.at[pl.ds(quad * 4, 4)],
            d_send2.at[2 * p + r],
            d_recv2.at[quad],
            device_id={"slot": same_place(owner_quad(p, r))},
            device_id_type=MESH,
        )

    def each_far_owner(act):
        for p, r in owners:

            @pl.when(quad != owner_quad(p, r))
            def _():
                act(p, r)

    for i in range(1, 4):
        near_decay(i).start()
    for p in range(PARTS):
        later_subs(p)
        for i in range(1, 4):
            to_quad(p, i).start()


    def to_owner(p, r):
        return pltpu.make_async_remote_copy(
            t_send.at[p, r],
            o_recv.at[quad],
            s2.at[p, r],
            r2.at[quad],
            device_id={"slot": same_place(owner_quad(p, r))},
            device_id_type=MESH,
        )

    def from_owner(q):
        return pltpu.make_async_remote_copy(
            o_send.at[q],
            g_recv.at[my_part, my_half],
            s3.at[q],
            r3.at[my_part, my_half],
            device_id={"slot": same_place(q)},
            device_id_type=MESH,
        )

    def to_member(p, i):
        return pltpu.make_async_remote_copy(
            p_send.at[p, (member + i) % 4],
            c_recv.at[p, member],
            s4.at[p, i],
            r4.at[p, i],
            device_id={"slot": quad_peer(i)},
            device_id_type=MESH,
        )

    def decay_of(p, i):
        return decay_near[p, i : i + 1, :]

    def quad_totals(p):
        for i in range(1, 4):
            to_quad(p, i).wait_recv()
        run = quad_state(p, 0)
        n_state[p, 0] = run
        for i in range(1, 4):
            new = quad_state(p, i)
            n_state[p, i] = new
            run = decay_of(p, i) * run + new
        run = run.astype(BF16)
        for r in range(2):
            t_send[p, r] = run[16 * r : 16 * r + 16]
            mine = owner_quad(p, r) == quad

            @pl.when(mine)
            def _():
                o_recv[quad] = t_send[p, r]

            @pl.when(jnp.logical_not(mine))
            def _():
                to_owner(p, r).start()

    def own():
        run = jnp.zeros((16, WIDE), F32)
        for q in range(QUADS):
            o_send[q] = run.astype(BF16)
            other = quad != q

            @pl.when(other)
            def _():
                from_owner(q).start()
                to_owner_of(q).wait_recv()

            fade = decay_wide[4 * q : 4 * q + 1, :]
            for i in range(1, 4):
                fade = fade * decay_wide[4 * q + i : 4 * q + i + 1, :]
            run = fade * run + o_recv[q].astype(F32)
        g_recv[my_part, my_half] = o_send[quad]

    def to_owner_of(q):
        return pltpu.make_async_remote_copy(
            t_send.at[0, 0],
            o_recv.at[q],
            s2.at[0, 0],
            r2.at[q],
            device_id={"slot": same_place(q)},
            device_id_type=MESH,
        )

    def members(p):
        for r in range(2):

            @pl.when(owner_quad(p, r) != quad)
            def _():
                pltpu.make_async_remote_copy(
                    o_send.at[0],
                    g_recv.at[p, r],
                    s3.at[0],
                    r3.at[p, r],
                    device_id={"slot": after},
                    device_id_type=MESH,
                ).wait_recv()

        run = g_recv[p].reshape(32, WIDE).astype(F32)
        for i in range(4):
            p_send[p, i] = run.astype(BF16)
            if i < 3:
                run = decay_of(p, i) * run + n_state[p, i]
        c_recv[p, member] = p_send[p, member]
        for i in range(1, 4):
            to_member(p, i).start()

    def local(p):
        z_copy(p).wait()
        matrix = widen_matrix(p, 32)
        skip_row = dot(rows_ref[48:64, :], matrix)[0:1]
        for c in range(subs):
            at = slice(c * SUB, (c + 1) * SUB)
            y = dot(left_ref[c], right_ref[p, c]) * dot(e_ref[at, :], matrix)
            y = y + skip_row * xconv[p, at, :].astype(F32)
            gate = silu(zs[p, at, :].astype(F32))
            y_ref[p, at, :] = y * gate
            g_ref[p, at, :] = dot(ef_ref[at, :], matrix) * gate

    def finish(p):
        for i in range(1, 4):
            to_member(p, i).wait_recv()
        carried = c_recv[p].reshape(STATE, WIDE)
        for c in range(subs):
            at = slice(c * SUB, (c + 1) * SUB)
            gated = y_ref[p, at, :] + g_ref[p, at, :] * dot(c_ref[at, :], carried)
            y_ref[p, at, :] = gated
            square = gated * gated
            sq_ref[at, :] += square[:, :128] + square[:, 128:]

    def second_pass(p, carry):
        add_subs(p)
        chain(p)
        local(p)
        return carry

    edge()
    lax.fori_loop(0, 2, second_pass, 0)
    near = jnp.zeros((8, 128), F32)
    for i in range(4):
        near = jnp.where(iota((8, 128), 0) == i, decay_all[quad * 4 + i], near)
    for p in range(PARTS):
        rest = near
        wide = jnp.zeros((8, WIDE), F32)
        r = iota((128, WIDE), 0)
        matrix = (r == 4 * p + iota((128, WIDE), 1) // HEAD_DIM).astype(F32).astype(BF16)
        for _ in range(3):
            term = rest.astype(BF16)
            rest = rest - term.astype(F32)
            wide = wide + dot(term, matrix)
        decay_near[p] = wide
    edge_rows()
    for p in range(PARTS):
        quad_totals(p)
    lax.fori_loop(2, PARTS, second_pass, 0)

    for halo in halos:
        halo.wait_send()
    for i in range(1, 4):
        near_decay(i).wait_send()
        edge_to(i).wait_send()
        for p in range(PARTS):
            to_quad(p, i).wait_send()
    each_far_owner(lambda p, r: far_decay(p, r).wait_send())

    @pl.when(is_owner)
    def _():
        for q in range(QUADS):

            @pl.when(quad != q)
            def _():
                pltpu.make_async_remote_copy(
                    decay_all.at[pl.ds(4 * q, 4)],
                    decay_all.at[pl.ds(4 * q, 4)],
                    d_send2.at[0],
                    d_recv2.at[q],
                    device_id={"slot": same_place(q)},
                    device_id_type=MESH,
                ).wait_recv()

        for k in range(slots):
            decay_rows[k : k + 1, :] = decay_all[k]
        rest = decay_rows[...]
        wide = jnp.zeros((slots, WIDE), F32)
        r = iota((128, WIDE), 0)
        matrix = (r == 4 * my_part + iota((128, WIDE), 1) // HEAD_DIM).astype(F32).astype(BF16)
        for _ in range(3):
            term = rest.astype(BF16)
            rest = rest - term.astype(F32)
            wide = wide + dot(term, matrix)
        decay_wide[...] = wide
        own()

    each_far_owner(lambda p, r: to_owner(p, r).wait_send())
    lax.fori_loop(0, PARTS, lambda p, c: (members(p), c)[1], 0)

    @pl.when(is_owner)
    def _():
        lax.fori_loop(1, QUADS, lambda i, c: (from_owner((quad + i) % QUADS).wait_send(), c)[1], 0)

    sq_ref[...] = jnp.zeros_like(sq_ref)
    lax.fori_loop(0, PARTS, lambda p, c: (finish(p), c)[1], 0)

    def over_columns(v):
        return lax.dot_general(
            jnp.ones((16, 128), BF16), v, (((1,), (1,)), ((), ())), preferred_element_type=F32
        )

    high = sq_ref[...].astype(BF16)
    low = (sq_ref[...] - high.astype(F32)).astype(BF16)
    sums = over_columns(high) + over_columns(low)
    n_send[0] = sums[0:1]
    n_recv[tp] = sums[0:1]

    def to_tp(i):
        return pltpu.make_async_remote_copy(
            n_send.at[0],
            n_recv.at[tp],
            ns.at[i],
            nr.at[i],
            device_id={"tp": (tp + i) % tp_size},
            device_id_type=MESH,
        )

    for i in range(1, tp_size):
        to_tp(i).start()
    for p in range(PARTS):
        for i in range(1, 4):
            to_member(p, i).wait_send()
    for i in range(1, tp_size):
        to_tp(i).wait_recv()
    everyone = n_recv[0]
    for k in range(1, tp_size):
        everyone = everyone + n_recv[k]
    scale = lax.rsqrt(everyone * (1.0 / (PARTS * WIDE * tp_size)) + EPSILON)
    high = scale.astype(BF16).astype(F32)
    row = iota((16, tokens), 0)
    terms = jnp.where(row == 0, high, jnp.where(row == 1, scale - high, 0.0)).astype(BF16)
    sq_ref[...] = lax.dot_general(
        terms, jnp.ones((16, 128), BF16), (((0,), (0,)), ((), ())), preferred_element_type=F32
    )

    for i in range(1, tp_size):
        to_tp(i).wait_send()


def write(y_ref, scale_ref, norm_ref, out_hbm, out_ref, sem):
    def copy(i):
        return pltpu.make_async_copy(out_ref.at[i], out_hbm.at[pl.ds(i * 128, 128)], sem.at[i])

    blocks = out_ref.shape[0]
    for i in range(blocks):
        at = slice(i * 128, (i + 1) * 128)
        scale = scale_ref[at, :]
        scale = jnp.concatenate([scale, scale], axis=1)
        for p in range(PARTS):
            out_ref[i, :, p * WIDE : (p + 1) * WIDE] = (y_ref[p, at, :] * scale * norm_ref[p]).astype(BF16)
        copy(i).start()
    for i in range(blocks):
        copy(i).wait()


def body(x_in, bc_in, z_gate, decay_rate, step_size, d_skip, conv_x, conv_bc, norm_weight, lengths):
    tokens, columns = x_in.shape
    subs = tokens // SUB
    tp_size = lax.axis_size("tp")
    heads = columns // HEAD_DIM
    vmem = pl.BlockSpec(memory_space=pltpu.VMEM)
    hbm = pl.BlockSpec(memory_space=pl.ANY)
    dma = pltpu.SemaphoreType.DMA
    split_taps = conv_x.reshape(4, PARTS, WIDE).transpose(1, 0, 2)
    gated, scale = pl.pallas_call(
        functools.partial(kernel, tp_size),
        out_shape=[pltpu.VMEM((PARTS, tokens, WIDE), F32), pltpu.VMEM((tokens, 128), F32)],
        in_specs=[hbm] * 9,
        out_specs=[vmem, vmem],
        scratch_shapes=[
            pltpu.SMEM((4,), jnp.int32),
            pltpu.VMEM((heads, tokens), F32),
            pltpu.VMEM((heads, tokens), F32),
            pltpu.VMEM((1, heads), F32),
            pltpu.VMEM((PARTS, 4, WIDE), F32),
            pltpu.VMEM((4, 2 * STATE), F32),
            pltpu.VMEM((PARTS, 16 + tokens, WIDE), BF16),
            pltpu.VMEM((PARTS, tokens, WIDE), BF16),
            pltpu.VMEM((PARTS, 32, WIDE), BF16),
            pltpu.VMEM((32, 2 * STATE), BF16),
            pltpu.VMEM((16 + tokens, 2 * STATE), BF16),
            pltpu.VMEM((-(-subs // 3), 576, 208), BF16),
            pltpu.VMEM((-(-subs // 4), 4 * STATE, 4 * SUB), BF16),
            pltpu.VMEM((subs, SUB, STATE + SUB), BF16),
            pltpu.VMEM((PARTS, subs, STATE + SUB, WIDE), BF16),
            pltpu.VMEM((tokens, STATE), BF16),
            pltpu.VMEM((PARTS, tokens, WIDE), BF16),
            pltpu.VMEM((tokens, 32), F32),
            pltpu.VMEM((tokens, 32), F32),
            pltpu.VMEM((PARTS, subs, STATE, WIDE), F32),
            pltpu.VMEM((3, 1, PARTS * WIDE + STATE), F32),
            pltpu.VMEM((12, 1, PARTS * WIDE + STATE), F32),
            pltpu.VMEM((4, 8, PARTS * WIDE + STATE), F32),
            pltpu.VMEM((PARTS, 4, 32, WIDE), F32),
            pltpu.VMEM((16, 32), F32),
            pltpu.VMEM((16, 32), F32),
            pltpu.VMEM((tokens, 32), BF16),
            pltpu.VMEM((tokens, 32), BF16),
            pltpu.VMEM((tokens, 32), BF16),
            pltpu.VMEM((tokens, 32), BF16),
            pltpu.VMEM((tokens, STATE), BF16),
            pltpu.VMEM((STATE, tokens), BF16),
            pltpu.VMEM((64, 32), BF16),
            pltpu.VMEM((PARTS, tokens, WIDE), F32),
            pltpu.VMEM((4 * QUADS, 1, 128), F32),
            pltpu.VMEM((4 * QUADS, 128), F32),
            pltpu.VMEM((4 * QUADS, WIDE), F32),
            pltpu.VMEM((PARTS, 8, WIDE), F32),
            pltpu.VMEM((PARTS, 4, 32, WIDE), BF16),
            pltpu.VMEM((PARTS, 4, 32, WIDE), BF16),
            pltpu.VMEM((PARTS, 2, 16, WIDE), BF16),
            pltpu.VMEM((QUADS, 16, WIDE), BF16),
            pltpu.VMEM((QUADS, 16, WIDE), BF16),
            pltpu.VMEM((PARTS, 2, 16, WIDE), BF16),
            pltpu.VMEM((PARTS, 4, 32, WIDE), BF16),
            pltpu.VMEM((PARTS, 4, 32, WIDE), BF16),
            pltpu.VMEM((1, 1, tokens), F32),
            pltpu.VMEM((tp_size, 1, tokens), F32),
            dma((2 * PARTS + 7,)),
            dma((PARTS + 1,)),
            dma((PARTS + 1,)),
            dma((4,)),
            dma((4,)),
            dma((4,)),
            dma((4,)),
            dma((QUADS,)),
            dma((QUADS,)),
            dma((PARTS, 4)),
            dma((PARTS, 4)),
            dma((PARTS, 4)),
            dma((QUADS,)),
            dma((QUADS,)),
            dma((PARTS, 4)),
            dma((PARTS, 4)),
            dma((PARTS, 4)),
            dma((tp_size,)),
            dma((tp_size,)),
        ],
        compiler_params=pltpu.CompilerParams(
            collective_id=0, has_side_effects=True, vmem_limit_bytes=56 * 1024 * 1024
        ),
    )(
        lengths,
        x_in,
        bc_in,
        z_gate,
        decay_rate.T,
        step_size.T,
        d_skip.reshape(1, heads),
        split_taps,
        conv_bc,
    )
    return pl.pallas_call(
        write,
        out_shape=jax.ShapeDtypeStruct((tokens, columns), BF16),
        in_specs=[vmem] * 3,
        out_specs=hbm,
        scratch_shapes=[pltpu.VMEM((tokens // 128, 128, columns), BF16), dma((tokens // 128,))],
        compiler_params=pltpu.CompilerParams(vmem_limit_bytes=8 * 1024 * 1024),
    )(gated, scale, norm_weight.reshape(PARTS, 1, WIDE))


def solution(mesh):
    placed = (
        P("slot", "tp"),
        P("slot", "tp"),
        P("slot", "tp"),
        P("slot", "tp"),
        P("slot", "tp"),
        P("tp"),
        P(None, "tp"),
        P(None, "tp"),
        P("tp"),
        P(),
    )
    return jax.shard_map(
        body, mesh=mesh, in_specs=placed, out_specs=P("slot", "tp"), check_vma=False
    )
```
